128 devices in a mesh: inst: 16 (over y_hi, x, core), tp: 8 (over y_lo, z).
Axes of the slice: x: 4, y: 4 (y_hi: 2, y_lo: 2; y = y_hi * 2 + y_lo), z: 4, core: 2. Of those that a mesh axis runs over, the one named last changes fastest.
Arguments:
- hidden: bfloat16 [4, 512, 8192], P(None, 'inst'), may hold values from -6 to 6
- query_weight: bfloat16 [8192, 4096], P(None, 'tp'), may hold values from -0.0625 to 0.0625
- output_weight: bfloat16 [4096, 8192], P('tp'), may hold values from -0.09375 to 0.09375
- kv_pool: bfloat16 [1536, 2, 64, 1024], P('inst', None, None, 'tp'), may hold values from -620 to 620
- new_kv: bfloat16 [4, 512, 2, 1024], P(None, 'inst', None, 'tp'), may hold values from -6 to 6
- lengths: int32 [512], P('inst'), may hold values from 1 to 192, as said below
- page_table: int32 [512, 3], P('inst'), may hold values from 0 to 95, as said below
- mig_req: int32 [256], P('inst'), may hold values from 0 to 31, as said below
- mig_dest: int32 [256, 1], P('inst'), may hold values from 0 to 15; in each aligned block of 16 rows (0 to 15, 16 to 31, ...) at most 2 rows name the same one
- resume: int32 [256], P('inst'), may hold values from 0 to 3
Outputs:
- home_out: bfloat16 [4, 512, 8192], P(None, 'inst', 'tp')
- arrival_out: bfloat16 [4, 512, 8192], P(None, 'inst', 'tp')
- arrival_cache: bfloat16 [512, 3, 2, 64, 1024], P('inst', None, None, None, 'tp')
The draws below stay inside these ranges and needn't reach their ends.
Inputs may be any that keep to these rules, and one draw needn't show every extreme that they name: Every draw has a request with exactly 192 cached tokens; typical lengths differ between instances by up to a factor of four. `page_table`: each instance's rows together name every page number of its pool exactly once. `mig_req`: the leaving requests of one instance are distinct. `mig_dest`: among the rows of one instance, no instance is named more than 2 times.
All inputs are finite; a program needn't handle non-finite values.
Results may differ from the reference program's by a relative error of at most 0.012.
Values may be sent and summed in bfloat16 or wider, within the bound.
No kernel may reach another device: no remote copies, remote signals or barrier semaphores. Data moves between devices by JAX's collectives and lax.ppermute only.
A program may use at most 128 MiB of HBM per device.

```python
import math
import jax
import jax.numpy as jnp
import numpy as np

D = 8192
HD = 128
GROUP = 4
STEPS = 4
PAGE = 64
CAP = 2
REQS = 32
MAXP = 3
KV_HEADS = 8
INSTANCES = 16
MIG = 16
ARRIVALS = 32
POOL = 96


def draw_kv_pool(key, part):
    key = jax.random.fold_in(key, 41)
    first = jax.random.fold_in(key, 0)
    count = INSTANCES * POOL
    shape = (count, 2, PAGE, KV_HEADS * HD)
    base = jnp.clip(jax.random.normal(first, shape, jnp.float32), -6.0, 6.0)
    return base.astype(jnp.bfloat16)


def draw_lengths(key, part):
    key = jax.random.fold_in(key, 11)
    first, second, third = jax.random.split(key, 3)
    longest = MAXP * PAGE
    load = jax.random.randint(first, (INSTANCES, 1), 1, 5)
    spread = jnp.maximum(load * longest // 4, 1)
    raw = jax.random.randint(second, (INSTANCES, REQS), 0, 1 << 20)
    values = (1 + raw % spread).reshape(-1)
    pick = jax.random.randint(third, (), 0, INSTANCES * REQS)
    marker = jnp.arange(INSTANCES * REQS, dtype=jnp.int32) == pick
    return jnp.where(marker, longest, values).astype(jnp.int32)


def draw_page_table(key, part):
    key = jax.random.fold_in(key, 23)
    keys = jax.random.split(key, INSTANCES)
    tables = jax.vmap(lambda single: jax.random.permutation(single, POOL))(keys)
    return tables.reshape(INSTANCES * REQS, MAXP).astype(jnp.int32)


def draw_mig_req(key, part):
    key = jax.random.fold_in(key, 37)
    keys = jax.random.split(key, INSTANCES)
    chosen = jax.vmap(lambda single: jax.random.permutation(single, REQS)[:MIG])(keys)
    return chosen.reshape(-1).astype(jnp.int32)


def touch_ends(array, stream_key, low, largest):
    spot = [jax.random.randint(jax.random.fold_in(stream_key, axis), (), 0, length) for axis, length in enumerate(array.shape)]
    widest = array.shape.index(max(array.shape))
    neighbour = spot[:widest] + [(spot[widest] + 1) % array.shape[widest]] + spot[widest + 1:]
    return array.at[tuple(spot)].set(low).at[tuple(neighbour)].set(largest)


def block_levels(key, dims, cuts, least, top_value):
    factor_of = 1.0
    for dim, parts in cuts:
        steps = jax.random.uniform(jax.random.fold_in(jax.random.fold_in(key, 6), dim), (parts,), jnp.float32, least / len(cuts), top_value / len(cuts))
        factor_of = factor_of * jnp.repeat(jnp.exp(steps), dims[dim] // parts).reshape((-1,) + (1,) * (len(dims) - 1 - dim))
    return factor_of


def routed_block(rng, own, number, rows, amount, top, limit, slope):
    sequence = jax.random.permutation(rng, amount)
    crowded, common = load_shares(amount, rows * top, limit, slope, True), load_shares(amount, rows * top, limit, slope, False)
    places = jnp.arange(amount)

    def named(sizes, turn):
        used = int((sizes > 0).sum())
        fixed = max(1, used // 4)
        shifted = fixed + (places - fixed + turn * (used - fixed)) % max(1, amount - fixed)
        return jnp.zeros((amount,), jnp.int32).at[sequence[jnp.where(places < fixed, places, shifted)]].set(jnp.asarray(sizes, jnp.int32))

    sizes = jnp.where(number % 4 == 0, named(crowded, number // 4), named(common, number - number // 4 - 1))
    mixed = jax.random.permutation(jax.random.fold_in(own, 3), amount)
    donor, sink = mixed[0:amount // 2 * 2:2], mixed[1:amount // 2 * 2:2]
    slack = jnp.minimum(sizes[donor] - 1, limit - sizes[sink]) // 2
    slack = jnp.where((donor == sequence[0]) | (sink == sequence[0]) | (sizes[sink] == 0), 0, jnp.maximum(slack, 0))
    shifted = jax.random.randint(jax.random.fold_in(own, 4), (amount // 2,), 0, 1 << 20) % (slack + 1)
    sizes = sizes.at[donor].add(-shifted).at[sink].add(shifted)
    labels = jnp.searchsorted(jnp.cumsum(sizes), jnp.arange(rows * top), side="right").astype(jnp.int32)
    grid = labels.reshape(top, rows).T
    grid = grid[jax.random.permutation(jax.random.fold_in(own, 1), rows)]
    turn = jax.random.randint(jax.random.fold_in(own, 2), (rows, 1), 0, top)
    return jnp.take_along_axis(grid, (jnp.arange(top)[None, :] + turn) % top, axis=1)


def load_shares(amount, total, reach, skew, full):
    portions = [(1 << 20) // math.isqrt(rank ** skew) + 1 for rank in range(1, amount + 1)]
    largest = reach if full else min(reach, max(-(-total // amount), total * portions[0] // sum(portions)))
    least = 1 if total - largest >= amount - 1 else 0
    counts, spare = [largest] + [least] * (amount - 1), total - largest - least * (amount - 1)
    while spare > 0:
        candidates = [i for i in range(1, amount) if counts[i] < largest] or [i for i in range(1, amount) if counts[i] < reach]
        pool, remaining = sum([portions[i] for i in candidates]), spare
        for i in candidates:
            more = min(reach - counts[i], max(1, remaining * portions[i] // pool), spare)
            counts[i] = counts[i] + more
            spare = spare - more
    return np.array(counts)


def scatter_about(own_key, extent, scale, reach, cuts=(), kind=jnp.bfloat16):
    values = jax.random.normal(own_key, extent, jnp.float32) * scale
    if len(cuts) > 0:
        values = block_levels(own_key, extent, cuts, -0.22, 0.18) * values
    return jnp.clip(values, min=-reach, max=reach).astype(kind)


def setup_inputs(seed: int = 0) -> dict:
    splits = jax.random.split(jax.random.key(seed), 11)
    hidden = scatter_about(splits[0], (STEPS, INSTANCES * REQS, D), 1.0, 6.0, ((1, 16),))
    query_weight = scatter_about(splits[1], (D, KV_HEADS * GROUP * HD), D ** -0.5, 0.0625, ((1, 8),))
    output_weight = scatter_about(splits[2], (KV_HEADS * GROUP * HD, D), (KV_HEADS * GROUP * HD) ** -0.5, 0.09375, ((0, 8),))
    kv_pool = draw_kv_pool(jax.random.fold_in(splits[10], 71), 0)
    new_kv = scatter_about(splits[4], (STEPS, INSTANCES * REQS, 2, KV_HEADS * HD), 1.0, 6.0, ((1, 16), (3, 8)))
    lengths = draw_lengths(jax.random.fold_in(splits[10], 71), 0)
    page_table = draw_page_table(jax.random.fold_in(splits[10], 71), 0)
    mig_req = draw_mig_req(jax.random.fold_in(splits[10], 71), 0)
    mig_dest_keys = jax.random.split(jax.random.fold_in(splits[8], 1), (INSTANCES * MIG) // MIG)
    mig_dest_turns = jax.random.permutation(jax.random.fold_in(splits[8], 3), (INSTANCES * MIG) // MIG)
    mig_dest = jax.vmap(lambda own, number: routed_block(jax.random.fold_in(splits[8], 2), own, number, MIG, INSTANCES, 1, CAP, 2))(mig_dest_keys, mig_dest_turns).reshape((INSTANCES * MIG, 1))
    resume = touch_ends(jax.random.randint(splits[9], (INSTANCES * MIG,), 0, STEPS), jax.random.fold_in(splits[9], 1), 0, STEPS - 1).astype(jnp.int32)
    return {"hidden": hidden, "query_weight": query_weight, "output_weight": output_weight, "kv_pool": kv_pool, "new_kv": new_kv, "lengths": lengths, "page_table": page_table, "mig_req": mig_req, "mig_dest": mig_dest, "resume": resume}


ROPE_BASE = 500000.0


def rotate(query, position):
    half = query.shape[-1] // 2
    inverse = ROPE_BASE ** (-jnp.arange(half, dtype=jnp.float32) * 2.0 / query.shape[-1])
    angles = position.astype(jnp.float32)[..., None] * inverse
    angles = jnp.concatenate([angles, angles], axis=-1)
    turned = jnp.concatenate([-query[..., half:], query[..., :half]], axis=-1)
    return query * jnp.cos(angles) + turned * jnp.sin(angles)


def attend(query, pages, length, fresh):
    count = pages.shape[0]
    depth = query.shape[-1]
    steps_n = query.shape[0]
    keys = pages[:, :, 0].reshape(count, -1, depth).astype(jnp.float32)
    values = pages[:, :, 1].reshape(count, -1, depth).astype(jnp.float32)
    query_wide = query.astype(jnp.float32)
    fresh_wide = fresh.astype(jnp.float32)
    scale = depth ** -0.5
    older = jnp.einsum("sbgd,bld->bsgl", query_wide, keys) * scale
    newer = jnp.einsum("sbgd,ubd->bsgu", query_wide, fresh_wide[:, :, 0]) * scale
    live = jnp.arange(keys.shape[1], dtype=jnp.int32)[None, :] < length[:, None]
    older = jnp.where(live[:, None, None, :], older, -1e30)
    step_ids = jnp.arange(steps_n, dtype=jnp.int32)
    causal = step_ids[None, :] <= step_ids[:, None]
    newer = jnp.where(causal[None, :, None, :], newer, -1e30)
    top = jnp.maximum(jnp.max(older, axis=-1), jnp.max(newer, axis=-1))[..., None]
    older_w = jnp.exp(older - top)
    newer_w = jnp.exp(newer - top)
    total = (jnp.sum(older_w, axis=-1) + jnp.sum(newer_w, axis=-1))[..., None]
    older_p = (older_w / total).astype(jnp.bfloat16).astype(jnp.float32)
    newer_p = (newer_w / total).astype(jnp.bfloat16).astype(jnp.float32)
    result = jnp.einsum("bsgl,bld->sbgd", older_p, values)
    result = result + jnp.einsum("bsgu,ubd->sbgd", newer_p, fresh_wide[:, :, 1])
    return result.astype(jnp.bfloat16).reshape(steps_n, count, -1)


def reference(hidden, query_weight, output_weight, kv_pool, new_kv, lengths, page_table, mig_req, mig_dest, resume):
    steps_n, rows, width = hidden.shape
    heads_kv = kv_pool.shape[-1] // HD
    query = jnp.dot(hidden.reshape(-1, width), query_weight, preferred_element_type=jnp.float32)
    query = query.reshape(steps_n, rows, heads_kv, GROUP, HD)
    position = lengths[None, :] + jnp.arange(steps_n, dtype=jnp.int32)[:, None]
    rotated = rotate(query, position[:, :, None, None]).astype(jnp.bfloat16)
    owner = jnp.arange(rows, dtype=jnp.int32) // REQS
    global_pages = (owner[:, None] * POOL + page_table).astype(jnp.int32)
    raw_pages = kv_pool[global_pages]
    pages = raw_pages.reshape(rows, MAXP, 2, PAGE, heads_kv, HD)
    fresh = new_kv.reshape(steps_n, rows, 2, heads_kv, HD)
    per_head = jax.vmap(attend, in_axes=(2, 4, None, 3), out_axes=2)(rotated, pages, lengths, fresh)
    attended = per_head.reshape(steps_n, rows, -1)
    leaving = INSTANCES * MIG
    home_index = ((jnp.arange(leaving, dtype=jnp.int32) // MIG) * REQS + mig_req).astype(jnp.int32)
    moved = jnp.full((rows,), steps_n, jnp.int32).at[home_index].set(resume)
    step_ids = jnp.arange(steps_n, dtype=jnp.int32)[:, None]
    zero_rows = jnp.zeros_like(attended)
    home_rows = jnp.where((step_ids < moved[None, :])[:, :, None], attended, zero_rows)
    home_out = jnp.dot(home_rows.reshape(-1, home_rows.shape[-1]), output_weight, preferred_element_type=jnp.float32)
    home_out = home_out.reshape(steps_n, rows, -1).astype(jnp.bfloat16)
    dest = mig_dest[:, 0].reshape(INSTANCES, MIG)
    order = jnp.arange(MIG, dtype=jnp.int32)
    same = dest[:, :, None] == dest[:, None, :]
    earlier = order[None, None, :] < order[None, :, None]
    rank = jnp.sum((same & earlier).astype(jnp.int32), axis=2)
    source = jnp.arange(INSTANCES, dtype=jnp.int32)[:, None]
    slot = (dest * ARRIVALS + source * CAP + rank).reshape(-1).astype(jnp.int32)
    arrival_cache = jnp.zeros((INSTANCES * ARRIVALS,) + raw_pages.shape[1:], raw_pages.dtype).at[slot].set(raw_pages[home_index])
    taken = attended[:, home_index]
    carried = jnp.where((step_ids >= resume[None, :])[:, :, None], taken, jnp.zeros_like(taken))
    arrival_rows = jnp.zeros((steps_n, INSTANCES * ARRIVALS, attended.shape[-1]), attended.dtype).at[:, slot].set(carried)
    arrival_out = jnp.dot(arrival_rows.reshape(-1, arrival_rows.shape[-1]), output_weight, preferred_element_type=jnp.float32)
    arrival_out = arrival_out.reshape(steps_n, INSTANCES * ARRIVALS, -1).astype(jnp.bfloat16)
    return home_out, arrival_out, arrival_cache
```

```python
import jax
import jax.numpy as jnp
import numpy as np
from jax import lax
from jax.experimental import pallas as pl
from jax.experimental.pallas import tpu as pltpu
from jax.sharding import PartitionSpec as P

HD = 128
GROUP = 4
CAP = 2
STEPS = 4
REQS = 32
MIG = 16
INST = 16
PAGE = 64
MAXP = 3
RING = 4
SPAN = MAXP * PAGE
ROWS = STEPS * REQS
WIDE = 256
ROPE_BASE = 500000.0
F32 = jnp.float32
BF16 = jnp.bfloat16
SMEM = pl.BlockSpec(memory_space=pltpu.SMEM)
VMEM = pl.BlockSpec(memory_space=pltpu.VMEM)
ANY = pl.BlockSpec(memory_space=pl.ANY)


def pack_kernel(table, mreq, mdest, resume, pool, send, pick, slot_req, count, zeros, wide, sem):
    zeros[...] = jnp.zeros_like(zeros)

    def clear(s, carry):
        slot_req[s] = -1
        return carry

    def fresh(d, carry):
        count[d] = 0
        return carry

    lax.fori_loop(0, INST * CAP, clear, 0)
    lax.fori_loop(0, INST, fresh, 0)

    def place(k, carry):
        d = mdest[k]
        c = count[d]
        count[d] = c + 1
        slot_req[d * CAP + c] = mreq[k]
        return carry

    lax.fori_loop(0, MIG, place, 0)

    def ship(s, carry):
        req = slot_req[s]

        @pl.when(req >= 0)
        def _():
            for p in range(MAXP):
                pltpu.make_async_copy(pool.at[table[req * MAXP + p]], send.at[s, p], sem).start()

        @pl.when(req < 0)
        def _():
            pltpu.make_async_copy(zeros, send.at[s], sem).start()

        return carry

    lax.fori_loop(0, INST * CAP, ship, 0)

    rows = lax.broadcasted_iota(jnp.int32, (2 * ROWS, ROWS), 0)
    cols = lax.broadcasted_iota(jnp.int32, (2 * ROWS, ROWS), 1)
    wide[...] = jnp.where(rows == cols, 1.0, 0.0).astype(F32)
    lane = lax.broadcasted_iota(jnp.int32, (1, ROWS), 1)

    def clear_count(d, carry):
        count[d] = 0
        return carry

    lax.fori_loop(0, INST, clear_count, 0)

    def choose(k, carry):
        d = mdest[k]
        c = count[d]
        count[d] = c + 1
        req = mreq[k]
        first = resume[k]
        for t in range(STEPS):
            at = t * REQS + req
            here = jnp.where(lane == at, 1.0, 0.0).astype(F32)
            stay = jnp.where(t < first, 1.0, 0.0).astype(F32)
            wide[pl.ds(at, 1), :] = here * stay
            wide[pl.ds(ROWS + d * (STEPS * CAP) + t * CAP + c, 1), :] = here * (1.0 - stay)
        return carry

    lax.fori_loop(0, MIG, choose, 0)
    pick[...] = wide[...].astype(BF16)
    pltpu.make_async_copy(send, send, sem).wait()


def attend_kernel(
    where, lengths, table, len_row, freq, hidden, wq, wo, pool, new_kv,
    near0, near1, near2, near3,
    x, q_w, o_w, kv, fresh, turned, scores, probs, mixed, outs, acc, x_sem, q_sem, o_sem, kv_sem, out_sem,
):
    chunks = x_sem.shape[0]
    depth = x.shape[1] // chunks
    share = outs.shape[-1]
    y, z = where[0], where[1]

    def load(k):
        cut = pl.ds(k * depth, depth)
        return (
            pltpu.make_async_copy(hidden.at[:, cut], x.at[:, cut], x_sem.at[k]),
            pltpu.make_async_copy(wq.at[cut], q_w.at[cut], q_sem.at[k]),
        )

    for k in range(chunks):
        for copy in load(k):
            copy.start()
    kv_copy = pltpu.make_async_copy(pool, kv, kv_sem)
    kv_copy.start()
    order = [(k, j) for k in (2, 1, 3, 0) for j in (1, 0)]

    def weight(i):
        k, j = order[i]
        n = lax.rem(y + j, 2) * RING + lax.rem(z + k, RING)
        cut = pl.ds(pl.multiple_of(n * share, share), share)
        return pltpu.make_async_copy(wo.at[:, cut], o_w.at[i], o_sem.at[i])

    for i in range(len(order)):
        weight(i).start()

    row = lax.broadcasted_iota(jnp.int32, (REQS * 16, ROWS * 2), 0)
    col = lax.broadcasted_iota(jnp.int32, (REQS * 16, ROWS * 2), 1)
    home = (row % 16) * (2 * REQS) + (row // 16) * 2
    source = new_kv[...]
    for j in range(2):
        choice = jnp.where((col == home + j) & (row % 16 < STEPS), 1.0, 0.0).astype(BF16)
        fresh[j] = jnp.dot(choice, source, preferred_element_type=F32).astype(BF16)

    at = lax.broadcasted_iota(jnp.int32, (ROWS, REQS), 0)
    req = lax.broadcasted_iota(jnp.int32, (ROWS, REQS), 1)
    base = jnp.sum(
        jnp.where(at % REQS == req, len_row[...].astype(F32), 0.0), axis=1, keepdims=True
    )
    step = (lax.broadcasted_iota(jnp.int32, (ROWS, 1), 0) // REQS).astype(F32)
    angles = (base + step) * freq[...]
    cos = jnp.cos(angles)
    sin = jnp.sin(angles)
    lane = lax.broadcasted_iota(jnp.int32, (ROWS, HD), 1)
    sin = jnp.where(lane < HD // 2, -sin, sin)

    for k in range(chunks):
        for copy in load(k):
            copy.wait()
        cut = pl.ds(k * depth, depth)
        part = jnp.dot(x[:, cut], q_w[cut], preferred_element_type=F32)
        if k == 0:
            acc[...] = part
        else:
            acc[...] += part

    for g in range(GROUP):
        head = acc[:, g * HD:(g + 1) * HD]
        turned[g * ROWS:(g + 1) * ROWS] = head * cos + pltpu.roll(head, HD // 2, 1) * sin

    kv_copy.wait()
    scale = HD ** -0.5
    spot = lax.broadcasted_iota(jnp.int32, (16, WIDE), 1)
    when = lax.broadcasted_iota(jnp.int32, (16, WIDE), 0) % STEPS
    causal = (spot >= SPAN) & (spot - SPAN <= when)
    rest = jnp.zeros((WIDE - SPAN - 16, HD), BF16)

    def pages(r, j):
        cached = [kv[table[r * MAXP + p], j] for p in range(MAXP)]
        return jnp.concatenate(cached + [fresh[j, r * 16:(r + 1) * 16], rest], axis=0)

    for r in range(REQS):
        query = turned[pl.ds(r, 16, stride=REQS), :].astype(BF16)
        found = lax.dot_general(
            query, pages(r, 0), (((1,), (1,)), ((), ())), preferred_element_type=F32
        ) * scale
        live = (spot < lengths[r]) | causal
        scores[r * 16:(r + 1) * 16] = jnp.where(live, found, -1e30)

    held = scores[...]
    top = jnp.max(held, axis=1, keepdims=True)
    raised = jnp.exp(held - top)
    total = jnp.sum(raised, axis=1, keepdims=True)
    probs[...] = (raised * (1.0 / total)).astype(BF16)

    for r in range(REQS):
        mixed[pl.ds(r, 16, stride=REQS), :] = jnp.dot(
            probs[r * 16:(r + 1) * 16], pages(r, 1), preferred_element_type=F32
        )

    rows = jnp.concatenate(
        [mixed[g * ROWS:(g + 1) * ROWS].astype(BF16) for g in range(GROUP)], axis=1
    )
    near = (near0, near1, near2, near3)
    stores = []
    for i, (k, j) in enumerate(order):
        weight(i).wait()
        outs[i] = jnp.dot(rows, o_w[i], preferred_element_type=F32).astype(BF16)
        store = pltpu.make_async_copy(outs.at[i], near[k].at[j], out_sem.at[i])
        store.start()
        stores.append(store)
    for store in stores:
        store.wait()


def sum_kernel(own, a, b, c, out):
    out[...] = (
        own[1].astype(F32) + a[1].astype(F32) + b[1].astype(F32) + c[1].astype(F32)
    ).astype(BF16)


def close_kernel(own, a, b, c, other, pick, home, slots):
    total = (
        own[0].astype(F32) + a[0].astype(F32) + b[0].astype(F32) + c[0].astype(F32)
        + other[...].astype(F32)
    ).astype(BF16)
    both = jnp.dot(pick[...], total, preferred_element_type=F32).astype(BF16)
    home[...] = both[:ROWS]
    slots[...] = both[ROWS:]


def local(
    hidden, query_weight, output_weight, kv_pool, new_kv,
    lengths, page_table, mig_req, mig_dest, resume,
):
    width = hidden.shape[-1]
    share = width // lax.axis_size("tp")
    table = page_table.reshape(-1)
    send, pick = pl.pallas_call(
        pack_kernel,
        out_shape=(
            jax.ShapeDtypeStruct((INST * CAP,) + (MAXP,) + kv_pool.shape[1:], BF16),
            jax.ShapeDtypeStruct((2 * ROWS, ROWS), BF16),
        ),
        in_specs=[SMEM] * 4 + [ANY],
        out_specs=(ANY, VMEM),
        scratch_shapes=[
            pltpu.SMEM((INST * CAP,), jnp.int32),
            pltpu.SMEM((INST,), jnp.int32),
            pltpu.VMEM((MAXP,) + kv_pool.shape[1:], BF16),
            pltpu.VMEM((2 * ROWS, ROWS), F32),
            pltpu.SemaphoreType.DMA,
        ],
        cost_estimate=pl.CostEstimate(flops=0, bytes_accessed=6 << 20, transcendentals=0),
        name="pack_pages",
    )(table, mig_req, mig_dest.reshape(-1), resume, kv_pool)
    arrival_cache = lax.all_to_all(send, "inst", split_axis=0, concat_axis=0, tiled=True)

    tp = lax.axis_index("tp")
    where = jnp.stack([tp // RING, tp % RING]).astype(jnp.int32)
    half = HD // 2
    inverse = np.float32(ROPE_BASE) ** (-np.arange(half, dtype=np.float32) * np.float32(2.0) / np.float32(HD))
    freq = jnp.asarray(np.concatenate([inverse, inverse])[None, :].astype(np.float32))
    chunks = 8
    near_shape = jax.ShapeDtypeStruct((2, ROWS, share), BF16)
    near = pl.pallas_call(
        attend_kernel,
        out_shape=(near_shape,) * RING,
        in_specs=[SMEM, SMEM, SMEM, VMEM, VMEM, ANY, ANY, ANY, ANY, VMEM],
        out_specs=(ANY,) * RING,
        scratch_shapes=[
            pltpu.VMEM((ROWS, width), BF16),
            pltpu.VMEM(query_weight.shape, BF16),
            pltpu.VMEM((2 * RING, GROUP * HD, share), BF16),
            pltpu.VMEM(kv_pool.shape, BF16),
            pltpu.VMEM((2, REQS * 16, HD), BF16),
            pltpu.VMEM((GROUP * ROWS, HD), F32),
            pltpu.VMEM((REQS * 16, WIDE), F32),
            pltpu.VMEM((REQS * 16, WIDE), BF16),
            pltpu.VMEM((GROUP * ROWS, HD), F32),
            pltpu.VMEM((2 * RING, ROWS, share), BF16),
            pltpu.VMEM((ROWS, GROUP * HD), F32),
            pltpu.SemaphoreType.DMA((chunks,)),
            pltpu.SemaphoreType.DMA((chunks,)),
            pltpu.SemaphoreType.DMA((2 * RING,)),
            pltpu.SemaphoreType.DMA,
            pltpu.SemaphoreType.DMA((2 * RING,)),
        ],
        compiler_params=pltpu.CompilerParams(vmem_limit_bytes=40 << 20),
        cost_estimate=pl.CostEstimate(flops=2_400_000_000, bytes_accessed=24 << 20, transcendentals=200_000),
        name="attend",
    )(
        where, lengths, table, lengths.reshape(1, REQS), freq,
        hidden.reshape(ROWS, width), query_weight, output_weight, kv_pool,
        new_kv.reshape(2 * ROWS, HD),
    )

    def shift(k):
        return [(s, (s // RING) * RING + (s + k) % RING) for s in range(2 * RING)]

    got = [lax.ppermute(near[k], "tp", shift(k)) for k in (2, 1, 3)]
    part = pl.pallas_call(
        sum_kernel,
        out_shape=jax.ShapeDtypeStruct((ROWS, share), BF16),
        in_specs=[VMEM] * 4,
        out_specs=VMEM,
        cost_estimate=pl.CostEstimate(flops=0, bytes_accessed=2 << 20, transcendentals=0),
        name="sum_ring",
    )(near[0], *got)
    other = lax.ppermute(part, "tp", [(s, (s + RING) % (2 * RING)) for s in range(2 * RING)])
    home, slots = pl.pallas_call(
        close_kernel,
        out_shape=(jax.ShapeDtypeStruct((ROWS, share), BF16),) * 2,
        in_specs=[VMEM] * 6,
        out_specs=(VMEM,) * 2,
        cost_estimate=pl.CostEstimate(flops=0, bytes_accessed=2 << 20, transcendentals=0),
        name="close",
    )(near[0], *got, other, pick)
    rows = lax.all_to_all(
        slots.reshape(INST, STEPS * CAP, share), "inst", split_axis=0, concat_axis=0, tiled=True
    )
    arrival = jnp.transpose(rows.reshape(INST, STEPS, CAP, share), (1, 0, 2, 3))
    return (
        home.reshape(STEPS, REQS, share),
        arrival.reshape(STEPS, INST * CAP, share),
        arrival_cache,
    )


def solution(mesh):
    in_specs = (
        P(None, "inst", None),
        P(None, "tp"),
        P("tp", None),
        P("inst", None, None, "tp"),
        P(None, "inst", None, "tp"),
        P("inst"),
        P("inst", None),
        P("inst"),
        P("inst", None),
        P("inst"),
    )
    out_specs = (P(None, "inst", "tp"), P(None, "inst", "tp"), P("inst", None, None, None, "tp"))
    return jax.shard_map(local, mesh=mesh, in_specs=in_specs, out_specs=out_specs, check_vma=False)
```

```python
import jax
import jax.numpy as jnp
import numpy as np
from jax import lax
from jax.experimental import pallas as pl
from jax.experimental.pallas import tpu as pltpu
from jax.sharding import PartitionSpec as P

HD = 128
GROUP = 4
CAP = 2
STEPS = 4
REQS = 32
MIG = 16
INST = 16
PAGE = 64
MAXP = 3
RING = 4
SPAN = MAXP * PAGE
ROWS = STEPS * REQS
WIDE = 256
ROPE_BASE = 500000.0
VMEM_LIMIT = 58 << 20
F32 = jnp.float32
BF16 = jnp.bfloat16
SMEM = pl.BlockSpec(memory_space=pltpu.SMEM)
VMEM = pl.BlockSpec(memory_space=pltpu.VMEM)
ANY = pl.BlockSpec(memory_space=pl.ANY)


def pack_kernel(table, mreq, mdest, resume, pool, send, pick, slot_req, count, kv, zeros, wide, kv_sem, sem):
    load = pltpu.make_async_copy(pool, kv, kv_sem)
    load.start()
    zeros[...] = jnp.zeros_like(zeros)

    def clear(s, carry):
        slot_req[s] = -1
        return carry

    def fresh(d, carry):
        count[d] = 0
        return carry

    lax.fori_loop(0, INST * CAP, clear, 0)
    lax.fori_loop(0, INST, fresh, 0)

    def place(k, carry):
        d = mdest[k]
        c = count[d]
        count[d] = c + 1
        slot_req[d * CAP + c] = mreq[k]
        return carry

    lax.fori_loop(0, MIG, place, 0)
    load.wait()

    def ship(s, carry):
        req = slot_req[s]

        @pl.when(req >= 0)
        def _():
            for p in range(MAXP):
                pltpu.make_async_copy(kv.at[table[req * MAXP + p]], send.at[s, p], sem).start()

        @pl.when(req < 0)
        def _():
            pltpu.make_async_copy(zeros, send.at[s], sem).start()

        return carry

    lax.fori_loop(0, INST * CAP, ship, 0)

    rows = lax.broadcasted_iota(jnp.int32, (2 * ROWS, ROWS), 0)
    cols = lax.broadcasted_iota(jnp.int32, (2 * ROWS, ROWS), 1)
    wide[...] = jnp.where(rows == cols, 1.0, 0.0).astype(F32)
    lane = lax.broadcasted_iota(jnp.int32, (1, ROWS), 1)

    def clear_count(d, carry):
        count[d] = 0
        return carry

    lax.fori_loop(0, INST, clear_count, 0)

    def choose(k, carry):
        d = mdest[k]
        c = count[d]
        count[d] = c + 1
        req = mreq[k]
        first = resume[k]
        for t in range(STEPS):
            at = t * REQS + req
            here = jnp.where(lane == at, 1.0, 0.0).astype(F32)
            stay = jnp.where(t < first, 1.0, 0.0).astype(F32)
            wide[pl.ds(at, 1), :] = here * stay
            wide[pl.ds(ROWS + d * (STEPS * CAP) + t * CAP + c, 1), :] = here * (1.0 - stay)
        return carry

    lax.fori_loop(0, MIG, choose, 0)
    pick[...] = wide[...].astype(BF16)
    pltpu.make_async_copy(send, send, sem).wait()


def attend_kernel(
    where, lengths, table, len_row, freq, hidden, wq, wo, pool, new_kv,
    near0, near1, near2, near3,
    x, q_w, o_w, kv, fresh, turned, scores, probs, mixed, outs, acc, x_sem, q_sem, o_sem, kv_sem, out_sem,
):
    chunks = x_sem.shape[0]
    depth = x.shape[1] // chunks
    share = outs.shape[-1]
    y, z = where[0], where[1]

    def load(k):
        cut = pl.ds(k * depth, depth)
        return (
            pltpu.make_async_copy(hidden.at[:, cut], x.at[:, cut], x_sem.at[k]),
            pltpu.make_async_copy(wq.at[cut], q_w.at[cut], q_sem.at[k]),
        )

    for k in range(chunks):
        for copy in load(k):
            copy.start()
    kv_copy = pltpu.make_async_copy(pool, kv, kv_sem)
    kv_copy.start()
    order = [(k, j) for k in (2, 1, 3, 0) for j in (1, 0)]

    def weight(i):
        k, j = order[i]
        n = lax.rem(y + j, 2) * RING + lax.rem(z + k, RING)
        cut = pl.ds(pl.multiple_of(n * share, share), share)
        return pltpu.make_async_copy(wo.at[:, cut], o_w.at[i], o_sem.at[i])

    for i in range(len(order)):
        weight(i).start()

    row = lax.broadcasted_iota(jnp.int32, (REQS * 16, ROWS * 2), 0)
    col = lax.broadcasted_iota(jnp.int32, (REQS * 16, ROWS * 2), 1)
    home = (row % 16) * (2 * REQS) + (row // 16) * 2
    source = new_kv[...]
    for j in range(2):
        choice = jnp.where((col == home + j) & (row % 16 < STEPS), 1.0, 0.0).astype(BF16)
        fresh[j] = jnp.dot(choice, source, preferred_element_type=F32).astype(BF16)

    at = lax.broadcasted_iota(jnp.int32, (ROWS, REQS), 0)
    req = lax.broadcasted_iota(jnp.int32, (ROWS, REQS), 1)
    base = jnp.sum(
        jnp.where(at % REQS == req, len_row[...].astype(F32), 0.0), axis=1, keepdims=True
    )
    step = (lax.broadcasted_iota(jnp.int32, (ROWS, 1), 0) // REQS).astype(F32)
    angles = (base + step) * freq[...]
    cos = jnp.cos(angles)
    sin = jnp.sin(angles)
    lane = lax.broadcasted_iota(jnp.int32, (ROWS, HD), 1)
    sin = jnp.where(lane < HD // 2, -sin, sin)

    for k in range(chunks):
        for copy in load(k):
            copy.wait()
        cut = pl.ds(k * depth, depth)
        part = jnp.dot(x[:, cut], q_w[cut], preferred_element_type=F32)
        if k == 0:
            acc[...] = part
        else:
            acc[...] += part

    for g in range(GROUP):
        head = acc[:, g * HD:(g + 1) * HD]
        turned[g * ROWS:(g + 1) * ROWS] = head * cos + pltpu.roll(head, HD // 2, 1) * sin

    kv_copy.wait()
    scale = HD ** -0.5
    spot = lax.broadcasted_iota(jnp.int32, (16, WIDE), 1)
    when = lax.broadcasted_iota(jnp.int32, (16, WIDE), 0) % STEPS
    causal = (spot >= SPAN) & (spot - SPAN <= when)
    rest = jnp.zeros((WIDE - SPAN - 16, HD), BF16)

    def pages(r, j):
        cached = [kv[table[r * MAXP + p], j] for p in range(MAXP)]
        return jnp.concatenate(cached + [fresh[j, r * 16:(r + 1) * 16], rest], axis=0)

    for r in range(REQS):
        query = turned[pl.ds(r, 16, stride=REQS), :].astype(BF16)
        found = lax.dot_general(
            query, pages(r, 0), (((1,), (1,)), ((), ())), preferred_element_type=F32
        ) * scale
        live = (spot < lengths[r]) | causal
        scores[r * 16:(r + 1) * 16] = jnp.where(live, found, -1e30)

    held = scores[...]
    top = jnp.max(held, axis=1, keepdims=True)
    raised = jnp.exp(held - top)
    total = jnp.sum(raised, axis=1, keepdims=True)
    probs[...] = (raised * (1.0 / total)).astype(BF16)

    for r in range(REQS):
        mixed[pl.ds(r, 16, stride=REQS), :] = jnp.dot(
            probs[r * 16:(r + 1) * 16], pages(r, 1), preferred_element_type=F32
        )

    rows = jnp.concatenate(
        [mixed[g * ROWS:(g + 1) * ROWS].astype(BF16) for g in range(GROUP)], axis=1
    )
    near = (near0, near1, near2, near3)
    stores = []
    for i, (k, j) in enumerate(order):
        weight(i).wait()
        outs[i] = jnp.dot(rows, o_w[i], preferred_element_type=F32).astype(BF16)
        store = pltpu.make_async_copy(outs.at[i], near[k].at[j], out_sem.at[i])
        store.start()
        stores.append(store)
    for store in stores:
        store.wait()


def sum_kernel(own, a, b, c, out):
    out[...] = (
        own[1].astype(F32) + a[1].astype(F32) + b[1].astype(F32) + c[1].astype(F32)
    ).astype(BF16)


def close_kernel(own, a, b, c, other, pick, home, slots):
    total = (
        own[0].astype(F32) + a[0].astype(F32) + b[0].astype(F32) + c[0].astype(F32)
        + other[...].astype(F32)
    ).astype(BF16)
    both = jnp.dot(pick[...], total, preferred_element_type=F32).astype(BF16)
    home[...] = both[:ROWS]
    slots[...] = both[ROWS:]


def local(
    hidden, query_weight, output_weight, kv_pool, new_kv,
    lengths, page_table, mig_req, mig_dest, resume,
):
    width = hidden.shape[-1]
    share = width // lax.axis_size("tp")
    table = page_table.reshape(-1)
    send, pick = pl.pallas_call(
        pack_kernel,
        out_shape=(
            jax.ShapeDtypeStruct((INST * CAP,) + (MAXP,) + kv_pool.shape[1:], BF16),
            jax.ShapeDtypeStruct((2 * ROWS, ROWS), BF16),
        ),
        in_specs=[SMEM] * 4 + [ANY],
        out_specs=(ANY, VMEM),
        scratch_shapes=[
            pltpu.SMEM((INST * CAP,), jnp.int32),
            pltpu.SMEM((INST,), jnp.int32),
            pltpu.VMEM(kv_pool.shape, BF16),
            pltpu.VMEM((MAXP,) + kv_pool.shape[1:], BF16),
            pltpu.VMEM((2 * ROWS, ROWS), F32),
            pltpu.SemaphoreType.DMA,
            pltpu.SemaphoreType.DMA,
        ],
        compiler_params=pltpu.CompilerParams(vmem_limit_bytes=VMEM_LIMIT),
        cost_estimate=pl.CostEstimate(flops=0, bytes_accessed=6 << 20, transcendentals=0),
        name="pack_pages",
    )(table, mig_req, mig_dest.reshape(-1), resume, kv_pool)
    arrival_cache = lax.all_to_all(send, "inst", split_axis=0, concat_axis=0, tiled=True)

    tp = lax.axis_index("tp")
    where = jnp.stack([tp // RING, tp % RING]).astype(jnp.int32)
    half = HD // 2
    inverse = np.float32(ROPE_BASE) ** (-np.arange(half, dtype=np.float32) * np.float32(2.0) / np.float32(HD))
    freq = jnp.asarray(np.concatenate([inverse, inverse])[None, :].astype(np.float32))
    chunks = 8
    near_shape = jax.ShapeDtypeStruct((2, ROWS, share), BF16)
    near = pl.pallas_call(
        attend_kernel,
        out_shape=(near_shape,) * RING,
        in_specs=[SMEM, SMEM, SMEM, VMEM, VMEM, ANY, ANY, ANY, ANY, VMEM],
        out_specs=(ANY,) * RING,
        scratch_shapes=[
            pltpu.VMEM((ROWS, width), BF16),
            pltpu.VMEM(query_weight.shape, BF16),
            pltpu.VMEM((2 * RING, GROUP * HD, share), BF16),
            pltpu.VMEM(kv_pool.shape, BF16),
            pltpu.VMEM((2, REQS * 16, HD), BF16),
            pltpu.VMEM((GROUP * ROWS, HD), F32),
            pltpu.VMEM((REQS * 16, WIDE), F32),
            pltpu.VMEM((REQS * 16, WIDE), BF16),
            pltpu.VMEM((GROUP * ROWS, HD), F32),
            pltpu.VMEM((2 * RING, ROWS, share), BF16),
            pltpu.VMEM((ROWS, GROUP * HD), F32),
            pltpu.SemaphoreType.DMA((chunks,)),
            pltpu.SemaphoreType.DMA((chunks,)),
            pltpu.SemaphoreType.DMA((2 * RING,)),
            pltpu.SemaphoreType.DMA,
            pltpu.SemaphoreType.DMA((2 * RING,)),
        ],
        compiler_params=pltpu.CompilerParams(vmem_limit_bytes=VMEM_LIMIT),
        cost_estimate=pl.CostEstimate(flops=2_400_000_000, bytes_accessed=24 << 20, transcendentals=200_000),
        name="attend",
    )(
        where, lengths, table, lengths.reshape(1, REQS), freq,
        hidden.reshape(ROWS, width), query_weight, output_weight, kv_pool,
        new_kv.reshape(2 * ROWS, HD),
    )

    def shift(k):
        return [(s, (s // RING) * RING + (s + k) % RING) for s in range(2 * RING)]

    got = [lax.ppermute(near[k], "tp", shift(k)) for k in (2, 1, 3)]
    part = pl.pallas_call(
        sum_kernel,
        out_shape=jax.ShapeDtypeStruct((ROWS, share), BF16),
        in_specs=[VMEM] * 4,
        out_specs=VMEM,
        cost_estimate=pl.CostEstimate(flops=0, bytes_accessed=2 << 20, transcendentals=0),
        name="sum_ring",
    )(near[0], *got)
    other = lax.ppermute(part, "tp", [(s, (s + RING) % (2 * RING)) for s in range(2 * RING)])
    home, slots = pl.pallas_call(
        close_kernel,
        out_shape=(jax.ShapeDtypeStruct((ROWS, share), BF16),) * 2,
        in_specs=[VMEM] * 6,
        out_specs=(VMEM,) * 2,
        cost_estimate=pl.CostEstimate(flops=0, bytes_accessed=2 << 20, transcendentals=0),
        name="close",
    )(near[0], *got, other, pick)
    arrival_cache, slots = lax.optimization_barrier((arrival_cache, slots))
    rows = lax.all_to_all(
        slots.reshape(INST, STEPS * CAP, share), "inst", split_axis=0, concat_axis=0, tiled=True
    )
    arrival = jnp.transpose(rows.reshape(INST, STEPS, CAP, share), (1, 0, 2, 3))
    return (
        home.reshape(STEPS, REQS, share),
        arrival.reshape(STEPS, INST * CAP, share),
        arrival_cache,
    )


def solution(mesh):
    in_specs = (
        P(None, "inst", None),
        P(None, "tp"),
        P("tp", None),
        P("inst", None, None, "tp"),
        P(None, "inst", None, "tp"),
        P("inst"),
        P("inst", None),
        P("inst"),
        P("inst", None),
        P("inst"),
    )
    out_specs = (P(None, "inst", "tp"), P(None, "inst", "tp"), P("inst", None, None, None, "tp"))
    return jax.shard_map(local, mesh=mesh, in_specs=in_specs, out_specs=out_specs, check_vma=False)
```

```python
import jax
import jax.numpy as jnp
import numpy as np
from jax import lax
from jax.experimental import pallas as pl
from jax.experimental.pallas import tpu as pltpu
from jax.sharding import PartitionSpec as P

HD = 128
GROUP = 4
CAP = 2
STEPS = 4
REQS = 32
MIG = 16
INST = 16
PAGE = 64
MAXP = 3
RING = 4
SPAN = MAXP * PAGE
ROWS = STEPS * REQS
WIDE = 256
ROPE_BASE = 500000.0
FULL_VMEM = 58 << 20
SMALL_VMEM = 6 << 20
F32 = jnp.float32
BF16 = jnp.bfloat16
SMEM = pl.BlockSpec(memory_space=pltpu.SMEM)
VMEM = pl.BlockSpec(memory_space=pltpu.VMEM)
ANY = pl.BlockSpec(memory_space=pl.ANY)


def pack_kernel(table, mreq, mdest, resume, pool, send, pick, slot_req, count, kv, zeros, wide, kv_sem, sem):
    load = pltpu.make_async_copy(pool, kv, kv_sem)
    load.start()
    zeros[...] = jnp.zeros_like(zeros)

    def clear(s, carry):
        slot_req[s] = -1
        return carry

    def fresh(d, carry):
        count[d] = 0
        return carry

    lax.fori_loop(0, INST * CAP, clear, 0)
    lax.fori_loop(0, INST, fresh, 0)

    def place(k, carry):
        d = mdest[k]
        c = count[d]
        count[d] = c + 1
        slot_req[d * CAP + c] = mreq[k]
        return carry

    lax.fori_loop(0, MIG, place, 0)
    load.wait()

    def ship(s, carry):
        req = slot_req[s]

        @pl.when(req >= 0)
        def _():
            for p in range(MAXP):
                pltpu.make_async_copy(kv.at[table[p, req]], send.at[s, p], sem).start()

        @pl.when(req < 0)
        def _():
            pltpu.make_async_copy(zeros, send.at[s], sem).start()

        return carry

    lax.fori_loop(0, INST * CAP, ship, 0)

    rows = lax.broadcasted_iota(jnp.int32, (2 * ROWS, ROWS), 0)
    cols = lax.broadcasted_iota(jnp.int32, (2 * ROWS, ROWS), 1)
    wide[...] = jnp.where(rows == cols, 1.0, 0.0).astype(F32)
    lane = lax.broadcasted_iota(jnp.int32, (1, ROWS), 1)

    def clear_count(d, carry):
        count[d] = 0
        return carry

    lax.fori_loop(0, INST, clear_count, 0)

    def choose(k, carry):
        d = mdest[k]
        c = count[d]
        count[d] = c + 1
        req = mreq[k]
        first = resume[k]
        for t in range(STEPS):
            at = t * REQS + req
            here = jnp.where(lane == at, 1.0, 0.0).astype(F32)
            stay = jnp.where(t < first, 1.0, 0.0).astype(F32)
            wide[pl.ds(at, 1), :] = here * stay
            wide[pl.ds(ROWS + d * (STEPS * CAP) + t * CAP + c, 1), :] = here * (1.0 - stay)
        return carry

    lax.fori_loop(0, MIG, choose, 0)
    pick[...] = wide[...].astype(BF16)
    pltpu.make_async_copy(send, send, sem).wait()


def attend_kernel(
    lengths, table, len_row, freq, hidden, wq, wo, pool, new_kv,
    near0, near1, near2, near3,
    x, q_w, o_w, kv, fresh, turned, scores, probs, mixed, outs, acc, x_sem, q_sem, o_sem, kv_sem, out_sem,
):
    chunks = x_sem.shape[0]
    depth = x.shape[1] // chunks
    share = outs.shape[-1]
    tp = lax.axis_index("tp")
    y, z = tp // RING, tp % RING

    def load(k):
        cut = pl.ds(k * depth, depth)
        return (
            pltpu.make_async_copy(hidden.at[:, cut], x.at[:, cut], x_sem.at[k]),
            pltpu.make_async_copy(wq.at[cut], q_w.at[cut], q_sem.at[k]),
        )

    for k in range(chunks):
        for copy in load(k):
            copy.start()
    kv_copy = pltpu.make_async_copy(pool, kv, kv_sem)
    order = [(k, j) for k in (2, 1, 3, 0) for j in (1, 0)]

    def weight(i):
        k, j = order[i]
        n = lax.rem(y + j, 2) * RING + lax.rem(z + k, RING)
        cut = pl.ds(pl.multiple_of(n * share, share), share)
        return pltpu.make_async_copy(wo.at[:, cut], o_w.at[i], o_sem.at[i])

    row = lax.broadcasted_iota(jnp.int32, (REQS * 16, ROWS * 2), 0)
    col = lax.broadcasted_iota(jnp.int32, (REQS * 16, ROWS * 2), 1)
    home = (row % 16) * (2 * REQS) + (row // 16) * 2
    source = new_kv[...]
    for j in range(2):
        choice = jnp.where((col == home + j) & (row % 16 < STEPS), 1.0, 0.0).astype(BF16)
        fresh[j] = jnp.dot(choice, source, preferred_element_type=F32).astype(BF16)

    at = lax.broadcasted_iota(jnp.int32, (ROWS, REQS), 0)
    req = lax.broadcasted_iota(jnp.int32, (ROWS, REQS), 1)
    base = jnp.sum(
        jnp.where(at % REQS == req, len_row[...].astype(F32), 0.0), axis=1, keepdims=True
    )
    step = (lax.broadcasted_iota(jnp.int32, (ROWS, 1), 0) // REQS).astype(F32)
    angles = (base + step) * freq[...]
    cos = jnp.cos(angles)
    sin = jnp.sin(angles)
    lane = lax.broadcasted_iota(jnp.int32, (ROWS, HD), 1)
    sin = jnp.where(lane < HD // 2, -sin, sin)

    for k in range(chunks):
        for copy in load(k):
            copy.wait()
        if k == 2:
            kv_copy.start()
        if k >= 4:
            for i in (2 * k - 8, 2 * k - 7):
                weight(i).start()
        cut = pl.ds(k * depth, depth)
        part = jnp.dot(x[:, cut], q_w[cut], preferred_element_type=F32)
        if k == 0:
            acc[...] = part
        else:
            acc[...] += part

    for g in range(GROUP):
        head = acc[:, g * HD:(g + 1) * HD]
        turned[g * ROWS:(g + 1) * ROWS] = head * cos + pltpu.roll(head, HD // 2, 1) * sin

    kv_copy.wait()
    scale = HD ** -0.5
    spot = lax.broadcasted_iota(jnp.int32, (16, WIDE), 1)
    when = lax.broadcasted_iota(jnp.int32, (16, WIDE), 0) % STEPS
    causal = (spot >= SPAN) & (spot - SPAN <= when)
    rest = jnp.zeros((WIDE - SPAN - 16, HD), BF16)

    def pages(r, j):
        cached = [kv[table[p, r], j] for p in range(MAXP)]
        return jnp.concatenate(cached + [fresh[j, r * 16:(r + 1) * 16], rest], axis=0)

    for r in range(REQS):
        query = turned[pl.ds(r, 16, stride=REQS), :].astype(BF16)
        found = lax.dot_general(
            query, pages(r, 0), (((1,), (1,)), ((), ())), preferred_element_type=F32
        ) * scale
        live = (spot < lengths[r]) | causal
        scores[r * 16:(r + 1) * 16] = jnp.where(live, found, -1e30)

    held = scores[...]
    top = jnp.max(held, axis=1, keepdims=True)
    raised = jnp.exp(held - top)
    total = jnp.sum(raised, axis=1, keepdims=True)
    probs[...] = (raised * (1.0 / total)).astype(BF16)

    for r in range(REQS):
        mixed[pl.ds(r, 16, stride=REQS), :] = jnp.dot(
            probs[r * 16:(r + 1) * 16], pages(r, 1), preferred_element_type=F32
        )

    rows = jnp.concatenate(
        [mixed[g * ROWS:(g + 1) * ROWS].astype(BF16) for g in range(GROUP)], axis=1
    )
    near = (near0, near1, near2, near3)
    stores = []
    for i, (k, j) in enumerate(order):
        weight(i).wait()
        outs[i] = jnp.dot(rows, o_w[i], preferred_element_type=F32).astype(BF16)
        store = pltpu.make_async_copy(outs.at[i], near[k].at[j], out_sem.at[i])
        store.start()
        stores.append(store)
    for store in stores:
        store.wait()


def sum_kernel(own, a, b, c, out):
    out[...] = (
        own[1].astype(F32) + a[1].astype(F32) + b[1].astype(F32) + c[1].astype(F32)
    ).astype(BF16)


def close_kernel(own, a, b, c, other, pick, home, slots):
    total = (
        own[0].astype(F32) + a[0].astype(F32) + b[0].astype(F32) + c[0].astype(F32)
        + other[...].astype(F32)
    ).astype(BF16)
    both = jnp.dot(pick[...], total, preferred_element_type=F32).astype(BF16)
    home[...] = both[:ROWS]
    slots[...] = both[ROWS:]


def arrive_kernel(rows, out):
    to = lax.broadcasted_iota(jnp.int32, (ROWS, ROWS), 0)
    come = lax.broadcasted_iota(jnp.int32, (ROWS, ROWS), 1)
    t, s, c = to // (INST * CAP), (to // CAP) % INST, to % CAP
    turn = jnp.where(come == s * (STEPS * CAP) + t * CAP + c, 1.0, 0.0).astype(BF16)
    out[...] = jnp.dot(turn, rows[...], preferred_element_type=F32).astype(BF16)


def copy_kernel(got, out):
    out[...] = got[...]


def local(
    hidden, query_weight, output_weight, kv_pool, new_kv,
    lengths, page_table, mig_req, mig_dest, resume,
):
    width = hidden.shape[-1]
    share = width // lax.axis_size("tp")
    table = page_table.T
    send, pick = pl.pallas_call(
        pack_kernel,
        out_shape=(
            jax.ShapeDtypeStruct((INST * CAP,) + (MAXP,) + kv_pool.shape[1:], BF16),
            jax.ShapeDtypeStruct((2 * ROWS, ROWS), BF16),
        ),
        in_specs=[SMEM] * 4 + [ANY],
        out_specs=(ANY, VMEM),
        scratch_shapes=[
            pltpu.SMEM((INST * CAP,), jnp.int32),
            pltpu.SMEM((INST,), jnp.int32),
            pltpu.VMEM(kv_pool.shape, BF16),
            pltpu.VMEM((MAXP,) + kv_pool.shape[1:], BF16),
            pltpu.VMEM((2 * ROWS, ROWS), F32),
            pltpu.SemaphoreType.DMA,
            pltpu.SemaphoreType.DMA,
        ],
        compiler_params=pltpu.CompilerParams(vmem_limit_bytes=FULL_VMEM),
        cost_estimate=pl.CostEstimate(flops=0, bytes_accessed=6 << 20, transcendentals=0),
        name="pack_pages",
    )(table, mig_req, mig_dest.reshape(-1), resume, kv_pool)
    arrival_cache = lax.all_to_all(send, "inst", split_axis=0, concat_axis=0, tiled=True)

    half = HD // 2
    inverse = np.float32(ROPE_BASE) ** (-np.arange(half, dtype=np.float32) * np.float32(2.0) / np.float32(HD))
    freq = jnp.asarray(np.concatenate([inverse, inverse])[None, :].astype(np.float32))
    chunks = 8
    near_shape = jax.ShapeDtypeStruct((2, ROWS, share), BF16)
    near = pl.pallas_call(
        attend_kernel,
        out_shape=(near_shape,) * RING,
        in_specs=[SMEM, SMEM, VMEM, VMEM, ANY, ANY, ANY, ANY, VMEM],
        out_specs=(ANY,) * RING,
        scratch_shapes=[
            pltpu.VMEM((ROWS, width), BF16),
            pltpu.VMEM(query_weight.shape, BF16),
            pltpu.VMEM((2 * RING, GROUP * HD, share), BF16),
            pltpu.VMEM(kv_pool.shape, BF16),
            pltpu.VMEM((2, REQS * 16, HD), BF16),
            pltpu.VMEM((GROUP * ROWS, HD), F32),
            pltpu.VMEM((REQS * 16, WIDE), F32),
            pltpu.VMEM((REQS * 16, WIDE), BF16),
            pltpu.VMEM((GROUP * ROWS, HD), F32),
            pltpu.VMEM((2 * RING, ROWS, share), BF16),
            pltpu.VMEM((ROWS, GROUP * HD), F32),
            pltpu.SemaphoreType.DMA((chunks,)),
            pltpu.SemaphoreType.DMA((chunks,)),
            pltpu.SemaphoreType.DMA((2 * RING,)),
            pltpu.SemaphoreType.DMA,
            pltpu.SemaphoreType.DMA((2 * RING,)),
        ],
        compiler_params=pltpu.CompilerParams(vmem_limit_bytes=FULL_VMEM),
        cost_estimate=pl.CostEstimate(flops=2_400_000_000, bytes_accessed=24 << 20, transcendentals=200_000),
        name="attend",
    )(
        lengths, table, lengths.reshape(1, REQS), freq,
        hidden.reshape(ROWS, width), query_weight, output_weight, kv_pool,
        new_kv.reshape(2 * ROWS, HD),
    )

    def shift(k):
        return [(s, (s // RING) * RING + (s + k) % RING) for s in range(2 * RING)]

    got = [lax.ppermute(near[k], "tp", shift(k)) for k in (2, 1, 3)]
    part = pl.pallas_call(
        sum_kernel,
        out_shape=jax.ShapeDtypeStruct((ROWS, share), BF16),
        in_specs=[VMEM] * 4,
        out_specs=VMEM,
        compiler_params=pltpu.CompilerParams(vmem_limit_bytes=SMALL_VMEM),
        cost_estimate=pl.CostEstimate(flops=0, bytes_accessed=2 << 20, transcendentals=0),
        name="sum_ring",
    )(near[0], *got)
    other = lax.ppermute(part, "tp", [(s, (s + RING) % (2 * RING)) for s in range(2 * RING)])
    home, slots = pl.pallas_call(
        close_kernel,
        out_shape=(jax.ShapeDtypeStruct((ROWS, share), BF16),) * 2,
        in_specs=[VMEM] * 6,
        out_specs=(VMEM,) * 2,
        compiler_params=pltpu.CompilerParams(vmem_limit_bytes=SMALL_VMEM),
        cost_estimate=pl.CostEstimate(flops=0, bytes_accessed=2 << 20, transcendentals=0),
        name="close",
    )(near[0], *got, other, pick)
    arrival_cache, slots = lax.optimization_barrier((arrival_cache, slots))
    rows = lax.all_to_all(
        slots.reshape(INST, STEPS * CAP, share), "inst", split_axis=0, concat_axis=0, tiled=True
    )
    arrival = pl.pallas_call(
        arrive_kernel,
        out_shape=jax.ShapeDtypeStruct((ROWS, share), BF16),
        in_specs=[VMEM],
        out_specs=VMEM,
        compiler_params=pltpu.CompilerParams(vmem_limit_bytes=SMALL_VMEM),
        name="arrive",
    )(rows.reshape(ROWS, share))
    block = pl.BlockSpec((4,) + arrival_cache.shape[1:], lambda i: (i, 0, 0, 0, 0))
    arrival_cache = pl.pallas_call(
        copy_kernel,
        out_shape=jax.ShapeDtypeStruct(arrival_cache.shape, BF16),
        grid=(INST * CAP // 4,),
        in_specs=[block],
        out_specs=block,
        compiler_params=pltpu.CompilerParams(vmem_limit_bytes=SMALL_VMEM),
        cost_estimate=pl.CostEstimate(flops=0, bytes_accessed=6 << 20, transcendentals=0),
        name="keep_pages",
    )(arrival_cache)
    return (
        home.reshape(STEPS, REQS, share),
        arrival.reshape(STEPS, INST * CAP, share),
        arrival_cache,
    )


def solution(mesh):
    in_specs = (
        P(None, "inst", None),
        P(None, "tp"),
        P("tp", None),
        P("inst", None, None, "tp"),
        P(None, "inst", None, "tp"),
        P("inst"),
        P("inst", None),
        P("inst"),
        P("inst", None),
        P("inst"),
    )
    out_specs = (P(None, "inst", "tp"), P(None, "inst", "tp"), P("inst", None, None, None, "tp"))
    return jax.shard_map(local, mesh=mesh, in_specs=in_specs, out_specs=out_specs, check_vma=False)
```

```python
import jax
import jax.numpy as jnp
import numpy as np
from jax import lax
from jax.experimental import pallas as pl
from jax.experimental.pallas import tpu as pltpu
from jax.sharding import PartitionSpec as P

HD = 128
GROUP = 4
CAP = 2
STEPS = 4
REQS = 32
MIG = 16
INST = 16
PAGE = 64
MAXP = 3
RING = 4
SPAN = MAXP * PAGE
ROWS = STEPS * REQS
WIDE = 256
ROPE_BASE = 500000.0
FULL_VMEM = 58 << 20
SMALL_VMEM = 6 << 20
F32 = jnp.float32
BF16 = jnp.bfloat16
SMEM = pl.BlockSpec(memory_space=pltpu.SMEM)
VMEM = pl.BlockSpec(memory_space=pltpu.VMEM)
ANY = pl.BlockSpec(memory_space=pl.ANY)


def pack_kernel(table, mreq, mdest, resume, pool, send, pick, slot_req, count, kv, zeros, wide, kv_sem, sem):
    load = pltpu.make_async_copy(pool, kv, kv_sem)
    load.start()
    zeros[...] = jnp.zeros_like(zeros)

    def clear(s, carry):
        slot_req[s] = -1
        return carry

    def fresh(d, carry):
        count[d] = 0
        return carry

    lax.fori_loop(0, INST * CAP, clear, 0)
    lax.fori_loop(0, INST, fresh, 0)

    def place(k, carry):
        d = mdest[k]
        c = count[d]
        count[d] = c + 1
        slot_req[d * CAP + c] = mreq[k]
        return carry

    lax.fori_loop(0, MIG, place, 0)
    rows = lax.broadcasted_iota(jnp.int32, (2 * ROWS, ROWS), 0)
    cols = lax.broadcasted_iota(jnp.int32, (2 * ROWS, ROWS), 1)
    wide[...] = jnp.where(rows == cols, 1.0, 0.0).astype(F32)
    lane = lax.broadcasted_iota(jnp.int32, (1, ROWS), 1)

    def clear_count(d, carry):
        count[d] = 0
        return carry

    lax.fori_loop(0, INST, clear_count, 0)

    def choose(k, carry):
        d = mdest[k]
        c = count[d]
        count[d] = c + 1
        req = mreq[k]
        first = resume[k]
        for t in range(STEPS):
            at = t * REQS + req
            here = jnp.where(lane == at, 1.0, 0.0).astype(F32)
            stay = jnp.where(t < first, 1.0, 0.0).astype(F32)
            wide[pl.ds(at, 1), :] = here * stay
            wide[pl.ds(ROWS + d * (STEPS * CAP) + t * CAP + c, 1), :] = here * (1.0 - stay)
        return carry

    lax.fori_loop(0, MIG, choose, 0)
    pick[...] = wide[...].astype(BF16)
    load.wait()

    def ship(s, carry):
        req = slot_req[s]

        @pl.when(req >= 0)
        def _():
            for p in range(MAXP):
                pltpu.make_async_copy(kv.at[table[p, req]], send.at[s, p], sem).start()

        @pl.when(req < 0)
        def _():
            pltpu.make_async_copy(zeros, send.at[s], sem).start()

        return carry

    lax.fori_loop(0, INST * CAP, ship, 0)

    pltpu.make_async_copy(send, send, sem).wait()


def attend_kernel(
    hidden, wq, wo, pool, new_kv, len_list, page_list, len_line, freq_line,
    far1, far0, up0, down1, up1, down0, own,
    x, q_w, o_w, kv, fresh, turned, scores, probs, mixed, outs, acc,
    recent, lengths, table, len_row, freq,
    x_sem, q_sem, o_sem, kv_sem, out_sem, small_sem,
):
    chunks = x_sem.shape[0]
    depth = x.shape[1] // chunks
    share = outs.shape[-1]
    tp = lax.axis_index("tp")
    y, z = tp // RING, tp % RING

    def load(k):
        cut = pl.ds(k * depth, depth)
        return (
            pltpu.make_async_copy(hidden.at[:, cut], x.at[:, cut], x_sem.at[k]),
            pltpu.make_async_copy(wq.at[cut], q_w.at[cut], q_sem.at[k]),
        )

    small = [
        pltpu.make_async_copy(source, target, small_sem.at[i])
        for i, (source, target) in enumerate((
            (new_kv, recent), (len_line, len_row), (freq_line, freq), (len_list, lengths), (page_list, table),
        ))
    ]
    for k in range(chunks):
        for copy in load(k):
            copy.start()
        if k == 0:
            for copy in small:
                copy.start()
    kv_copy = pltpu.make_async_copy(pool, kv, kv_sem)
    order = [(2, 1), (2, 0), (1, 0), (3, 1), (1, 1), (3, 0), (0, 1), (0, 0)]
    into = (far1, far0, up0, down1, up1, down0, own.at[1], own.at[0])

    def weight(i):
        k, j = order[i]
        n = lax.rem(y + j, 2) * RING + lax.rem(z + k, RING)
        cut = pl.ds(pl.multiple_of(n * share, share), share)
        return pltpu.make_async_copy(wo.at[:, cut], o_w.at[i], o_sem.at[i])

    for copy in small:
        copy.wait()

    row = lax.broadcasted_iota(jnp.int32, (REQS * 16, ROWS * 2), 0)
    col = lax.broadcasted_iota(jnp.int32, (REQS * 16, ROWS * 2), 1)
    home = (row & 15) * (2 * REQS) + (row >> 4) * 2
    source = recent[...]
    for j in range(2):
        choice = jnp.where((col == home + j) & ((row & 15) < STEPS), 1.0, 0.0).astype(BF16)
        fresh[j] = jnp.dot(choice, source, preferred_element_type=F32).astype(BF16)

    at = lax.broadcasted_iota(jnp.int32, (ROWS, REQS), 0)
    req = lax.broadcasted_iota(jnp.int32, (ROWS, REQS), 1)
    base = jnp.sum(
        jnp.where((at & (REQS - 1)) == req, len_row[...].astype(F32), 0.0), axis=1, keepdims=True
    )
    step = (lax.broadcasted_iota(jnp.int32, (ROWS, 1), 0) >> 5).astype(F32)
    angles = (base + step) * freq[...]
    cos = jnp.cos(angles)
    sin = jnp.sin(angles)
    lane = lax.broadcasted_iota(jnp.int32, (ROWS, HD), 1)
    sin = jnp.where(lane < HD // 2, -sin, sin)

    for k in range(chunks):
        for copy in load(k):
            copy.wait()
        if k == 2:
            kv_copy.start()
        if k >= 4:
            for i in (2 * k - 8, 2 * k - 7):
                weight(i).start()
        cut = pl.ds(k * depth, depth)
        part = jnp.dot(x[:, cut], q_w[cut], preferred_element_type=F32)
        if k == 0:
            acc[...] = part
        else:
            acc[...] += part

    for g in range(GROUP):
        head = acc[:, g * HD:(g + 1) * HD]
        turned[g * ROWS:(g + 1) * ROWS] = head * cos + pltpu.roll(head, HD // 2, 1) * sin

    kv_copy.wait()
    scale = HD ** -0.5
    spot = lax.broadcasted_iota(jnp.int32, (16, WIDE), 1)
    when = lax.broadcasted_iota(jnp.int32, (16, WIDE), 0) & (STEPS - 1)
    causal = (spot >= SPAN) & (spot - SPAN <= when)
    rest = jnp.zeros((WIDE - SPAN - 16, HD), BF16)

    def pages(r, j):
        cached = [kv[table[p, r], j] for p in range(MAXP)]
        return jnp.concatenate(cached + [fresh[j, r * 16:(r + 1) * 16], rest], axis=0)

    for r in range(REQS):
        query = turned[pl.ds(r, 16, stride=REQS), :].astype(BF16)
        found = lax.dot_general(
            query, pages(r, 0), (((1,), (1,)), ((), ())), preferred_element_type=F32
        ) * scale
        live = (spot < lengths[r]) | causal
        scores[r * 16:(r + 1) * 16] = jnp.where(live, found, -1e30)

    held = scores[...]
    top = jnp.max(held, axis=1, keepdims=True)
    raised = jnp.exp(held - top)
    total = jnp.sum(raised, axis=1, keepdims=True)
    probs[...] = (raised * (1.0 / total)).astype(BF16)

    for r in range(REQS):
        mixed[pl.ds(r, 16, stride=REQS), :] = jnp.dot(
            probs[r * 16:(r + 1) * 16], pages(r, 1), preferred_element_type=F32
        )

    rows = jnp.concatenate(
        [mixed[g * ROWS:(g + 1) * ROWS].astype(BF16) for g in range(GROUP)], axis=1
    )
    stores = []
    for i in range(len(order)):
        weight(i).wait()
        outs[i] = jnp.dot(rows, o_w[i], preferred_element_type=F32).astype(BF16)
        store = pltpu.make_async_copy(outs.at[i], into[i], out_sem.at[i])
        store.start()
        stores.append(store)
    for store in stores:
        store.wait()


def relay_kernel(up1, down0, far1, far0, next_up, next_down):
    next_up[...] = (up1[...].astype(F32) + far1[...].astype(F32)).astype(BF16)
    next_down[...] = (down0[...].astype(F32) + far0[...].astype(F32)).astype(BF16)


def close_kernel(own, up0, up1, down0, down1, pick, keep, pass_on, slots):
    y = lax.axis_index("tp") // RING
    near = own[0].astype(F32) + up0[...].astype(F32) + down0[...].astype(F32)
    other = (own[1].astype(F32) + up1[...].astype(F32) + down1[...].astype(F32)).astype(BF16)
    keep[...] = near
    pass_on[...] = other
    choice = pick[ROWS:]
    for j, part in enumerate((near.astype(BF16), other)):
        taken = jnp.dot(choice, part, preferred_element_type=F32).astype(BF16)
        slots[:, lax.rem(y + j, 2)] = taken.reshape(INST, STEPS * CAP, taken.shape[-1])


def home_kernel(keep, other, pick, home):
    total = (keep[...] + other[...].astype(F32)).astype(BF16)
    home[...] = jnp.dot(pick[:ROWS], total, preferred_element_type=F32).astype(BF16)


def arrive_kernel(rows, out):
    total = rows[:, 0].astype(F32) + rows[:, 1].astype(F32)
    total = total.reshape(ROWS, total.shape[-1]).astype(BF16)
    to = lax.broadcasted_iota(jnp.int32, (ROWS, ROWS), 0)
    come = lax.broadcasted_iota(jnp.int32, (ROWS, ROWS), 1)
    t, s, c = to >> 5, (to >> 1) & (INST - 1), to & (CAP - 1)
    turn = jnp.where(come == s * (STEPS * CAP) + t * CAP + c, 1.0, 0.0).astype(BF16)
    out[...] = jnp.dot(turn, total, preferred_element_type=F32).astype(BF16)


def copy_kernel(got, out):
    out[...] = got[...]


def local(
    hidden, query_weight, output_weight, kv_pool, new_kv,
    lengths, page_table, mig_req, mig_dest, resume,
):
    width = hidden.shape[-1]
    share = width // lax.axis_size("tp")
    table = page_table.T
    send, pick = pl.pallas_call(
        pack_kernel,
        out_shape=(
            jax.ShapeDtypeStruct((INST * CAP,) + (MAXP,) + kv_pool.shape[1:], BF16),
            jax.ShapeDtypeStruct((2 * ROWS, ROWS), BF16),
        ),
        in_specs=[SMEM] * 4 + [ANY],
        out_specs=(ANY, VMEM),
        scratch_shapes=[
            pltpu.SMEM((INST * CAP,), jnp.int32),
            pltpu.SMEM((INST,), jnp.int32),
            pltpu.VMEM(kv_pool.shape, BF16),
            pltpu.VMEM((MAXP,) + kv_pool.shape[1:], BF16),
            pltpu.VMEM((2 * ROWS, ROWS), F32),
            pltpu.SemaphoreType.DMA,
            pltpu.SemaphoreType.DMA,
        ],
        compiler_params=pltpu.CompilerParams(vmem_limit_bytes=FULL_VMEM),
        cost_estimate=pl.CostEstimate(flops=0, bytes_accessed=6 << 20, transcendentals=0),
        name="pack_pages",
    )(table, mig_req, mig_dest.reshape(-1), resume, kv_pool)
    arrival_cache = lax.all_to_all(send, "inst", split_axis=0, concat_axis=0, tiled=True)

    half = HD // 2
    inverse = np.float32(ROPE_BASE) ** (-np.arange(half, dtype=np.float32) * np.float32(2.0) / np.float32(HD))
    freq = jnp.asarray(np.concatenate([inverse, inverse])[None, :].astype(np.float32))
    chunks = 8
    piece = jax.ShapeDtypeStruct((ROWS, share), BF16)
    far1, far0, up0, down1, up1, down0, own = pl.pallas_call(
        attend_kernel,
        out_shape=(piece,) * 6 + (jax.ShapeDtypeStruct((2, ROWS, share), BF16),),
        in_specs=[ANY] * 9,
        out_specs=(ANY,) * 7,
        scratch_shapes=[
            pltpu.VMEM((ROWS, width), BF16),
            pltpu.VMEM(query_weight.shape, BF16),
            pltpu.VMEM((2 * RING, GROUP * HD, share), BF16),
            pltpu.VMEM(kv_pool.shape, BF16),
            pltpu.VMEM((2, REQS * 16, HD), BF16),
            pltpu.VMEM((GROUP * ROWS, HD), F32),
            pltpu.VMEM((REQS * 16, WIDE), F32),
            pltpu.VMEM((REQS * 16, WIDE), BF16),
            pltpu.VMEM((GROUP * ROWS, HD), F32),
            pltpu.VMEM((2 * RING, ROWS, share), BF16),
            pltpu.VMEM((ROWS, GROUP * HD), F32),
            pltpu.VMEM((2 * ROWS, HD), BF16),
            pltpu.SMEM((REQS,), jnp.int32),
            pltpu.SMEM((MAXP, REQS), jnp.int32),
            pltpu.VMEM((1, REQS), jnp.int32),
            pltpu.VMEM((1, HD), F32),
            pltpu.SemaphoreType.DMA((chunks,)),
            pltpu.SemaphoreType.DMA((chunks,)),
            pltpu.SemaphoreType.DMA((2 * RING,)),
            pltpu.SemaphoreType.DMA,
            pltpu.SemaphoreType.DMA((2 * RING,)),
            pltpu.SemaphoreType.DMA((5,)),
        ],
        compiler_params=pltpu.CompilerParams(vmem_limit_bytes=FULL_VMEM),
        cost_estimate=pl.CostEstimate(flops=2_400_000_000, bytes_accessed=24 << 20, transcendentals=200_000),
        name="attend",
    )(
        hidden.reshape(ROWS, width), query_weight, output_weight, kv_pool,
        new_kv.reshape(2 * ROWS, HD), lengths, table, lengths.reshape(1, REQS), freq,
    )

    def shift(k):
        return [(s, (s // RING) * RING + (s + k) % RING) for s in range(2 * RING)]

    def small(kernel, out, name):
        return pl.pallas_call(
            kernel,
            out_shape=out,
            compiler_params=pltpu.CompilerParams(vmem_limit_bytes=SMALL_VMEM),
            cost_estimate=pl.CostEstimate(flops=0, bytes_accessed=2 << 20, transcendentals=0),
            name=name,
        )

    far1 = lax.ppermute(far1, "tp", shift(1))
    far0 = lax.ppermute(far0, "tp", shift(-1))
    up0 = lax.ppermute(up0, "tp", shift(1))
    down1 = lax.ppermute(down1, "tp", shift(-1))
    next_up, next_down = small(relay_kernel, (piece,) * 2, "relay")(up1, down0, far1, far0)
    up1 = lax.ppermute(next_up, "tp", shift(1))
    down0 = lax.ppermute(next_down, "tp", shift(-1))
    keep, pass_on, slots = small(
        close_kernel,
        (
            jax.ShapeDtypeStruct((ROWS, share), F32),
            piece,
            jax.ShapeDtypeStruct((INST, 2, STEPS * CAP, share), BF16),
        ),
        "close",
    )(own, up0, up1, down0, down1, pick)
    other = lax.ppermute(pass_on, "tp", [(s, (s + RING) % (2 * RING)) for s in range(2 * RING)])
    arrival_cache, slots, other = lax.optimization_barrier((arrival_cache, slots, other))
    home = small(home_kernel, piece, "home")(keep, other, pick)
    peers = [
        [i * 2 * RING + y * RING + z for i in range(INST) for y in range(2)] for z in range(RING)
    ]
    rows = lax.all_to_all(
        slots.reshape(2 * INST, STEPS * CAP, share), ("inst", "tp"),
        split_axis=0, concat_axis=0, tiled=True, axis_index_groups=peers,
    )
    arrival = small(arrive_kernel, piece, "arrive")(rows.reshape(INST, 2, STEPS * CAP, share))
    block = pl.BlockSpec((4,) + arrival_cache.shape[1:], lambda i: (i, 0, 0, 0, 0))
    arrival_cache = pl.pallas_call(
        copy_kernel,
        out_shape=jax.ShapeDtypeStruct(arrival_cache.shape, BF16),
        grid=(INST * CAP // 4,),
        in_specs=[block],
        out_specs=block,
        compiler_params=pltpu.CompilerParams(vmem_limit_bytes=SMALL_VMEM),
        cost_estimate=pl.CostEstimate(flops=0, bytes_accessed=6 << 20, transcendentals=0),
        name="keep_pages",
    )(arrival_cache)
    return (
        home.reshape(STEPS, REQS, share),
        arrival.reshape(STEPS, INST * CAP, share),
        arrival_cache,
    )


def solution(mesh):
    in_specs = (
        P(None, "inst", None),
        P(None, "tp"),
        P("tp", None),
        P("inst", None, None, "tp"),
        P(None, "inst", None, "tp"),
        P("inst"),
        P("inst", None),
        P("inst"),
        P("inst", None),
        P("inst"),
    )
    out_specs = (P(None, "inst", "tp"), P(None, "inst", "tp"), P("inst", None, None, None, "tp"))
    return jax.shard_map(local, mesh=mesh, in_specs=in_specs, out_specs=out_specs, check_vma=False)
```

```python
import functools

import jax
import jax.numpy as jnp
import numpy as np
from jax import lax
from jax.experimental import pallas as pl
from jax.experimental.pallas import tpu as pltpu
from jax.sharding import PartitionSpec as P

HD = 128
GROUP = 4
CAP = 2
STEPS = 4
REQS = 32
MIG = 16
INST = 16
PAGE = 64
MAXP = 3
RING = 4
SPAN = MAXP * PAGE
ROWS = STEPS * REQS
WIDE = 256
ROPE_BASE = 500000.0
FULL_VMEM = 48 << 20
SMALL_VMEM = 6 << 20
F32 = jnp.float32
BF16 = jnp.bfloat16
SMEM = pl.BlockSpec(memory_space=pltpu.SMEM)
VMEM = pl.BlockSpec(memory_space=pltpu.VMEM)
ANY = pl.BlockSpec(memory_space=pl.ANY)


def pack_kernel(
    page_list, req_list, dest_list, resume_list, pool, send, pick,
    table, mreq, mdest, resume, slot_req, count, kv, zeros, wide, kv_sem, sem, small_sem,
):
    load = pltpu.make_async_copy(pool, kv, kv_sem)
    load.start()
    small = [
        pltpu.make_async_copy(source, target, small_sem.at[i])
        for i, (source, target) in enumerate((
            (req_list, mreq), (dest_list, mdest), (resume_list, resume), (page_list, table),
        ))
    ]
    for copy in small:
        copy.start()
    zeros[...] = jnp.zeros_like(zeros)

    def clear(s, carry):
        slot_req[s] = -1
        return carry

    def fresh(d, carry):
        count[d] = 0
        return carry

    lax.fori_loop(0, INST * CAP, clear, 0)
    lax.fori_loop(0, INST, fresh, 0)

    for copy in small:
        copy.wait()

    def place(k, carry):
        d = mdest[k]
        c = count[d]
        count[d] = c + 1
        slot_req[d * CAP + c] = mreq[k]
        return carry

    lax.fori_loop(0, MIG, place, 0)
    rows = lax.broadcasted_iota(jnp.int32, (2 * ROWS, ROWS), 0)
    cols = lax.broadcasted_iota(jnp.int32, (2 * ROWS, ROWS), 1)
    wide[...] = jnp.where(rows == cols, 1.0, 0.0).astype(F32)
    lane = lax.broadcasted_iota(jnp.int32, (1, ROWS), 1)

    def clear_count(d, carry):
        count[d] = 0
        return carry

    lax.fori_loop(0, INST, clear_count, 0)

    def choose(k, carry):
        d = mdest[k]
        c = count[d]
        count[d] = c + 1
        req = mreq[k]
        first = resume[k]
        for t in range(STEPS):
            at = t * REQS + req
            here = jnp.where(lane == at, 1.0, 0.0).astype(F32)
            stay = jnp.where(t < first, 1.0, 0.0).astype(F32)
            wide[pl.ds(at, 1), :] = here * stay
            wide[pl.ds(ROWS + d * (STEPS * CAP) + t * CAP + c, 1), :] = here * (1.0 - stay)
        return carry

    lax.fori_loop(0, MIG, choose, 0)
    pick[...] = wide[...].astype(BF16)
    load.wait()

    def ship(s, carry):
        req = slot_req[s]

        @pl.when(req >= 0)
        def _():
            for p in range(MAXP):
                pltpu.make_async_copy(kv.at[table[p, req]], send.at[s, p], sem).start()

        @pl.when(req < 0)
        def _():
            pltpu.make_async_copy(zeros, send.at[s], sem).start()

        return carry

    lax.fori_loop(0, INST * CAP, ship, 0)

    pltpu.make_async_copy(send, send, sem).wait()


def attend_kernel(
    hidden, wq, wo, pool, new_kv, len_list, page_list, len_line, freq_line,
    far1, far0, up0, down1, up1, down0, own,
    x, q_w, o_w, kv, fresh, turned, scores, probs, mixed, acc,
    recent, lengths, table, len_row, freq,
    x_sem, q_sem, o_sem, kv_sem, small_sem,
):
    chunks = x_sem.shape[0]
    depth = x.shape[1] // chunks
    share = own.shape[-1]
    tp = lax.axis_index("tp")
    y, z = tp // RING, tp % RING

    def load(k):
        cut = pl.ds(k * depth, depth)
        return (
            pltpu.make_async_copy(hidden.at[:, cut], x.at[:, cut], x_sem.at[k]),
            pltpu.make_async_copy(wq.at[cut], q_w.at[cut], q_sem.at[k]),
        )

    small = [
        pltpu.make_async_copy(source, target, small_sem.at[i])
        for i, (source, target) in enumerate((
            (new_kv, recent), (len_line, len_row), (freq_line, freq), (len_list, lengths), (page_list, table),
        ))
    ]
    for k in range(chunks):
        for copy in load(k):
            copy.start()
        if k == 0:
            for copy in small:
                copy.start()
    kv_copy = pltpu.make_async_copy(pool, kv, kv_sem)
    order = [(2, 1), (2, 0), (1, 0), (3, 1), (1, 1), (3, 0), (0, 1), (0, 0)]
    into = (far1, far0, up0, down1, up1, down0, own.at[1], own.at[0])

    def weight(i):
        k, j = order[i]
        n = lax.rem(y + j, 2) * RING + lax.rem(z + k, RING)
        cut = pl.ds(pl.multiple_of(n * share, share), share)
        return pltpu.make_async_copy(wo.at[:, cut], o_w.at[i], o_sem.at[i])

    for copy in small:
        copy.wait()

    row = lax.broadcasted_iota(jnp.int32, (REQS * 16, ROWS * 2), 0)
    col = lax.broadcasted_iota(jnp.int32, (REQS * 16, ROWS * 2), 1)
    home = (row & 15) * (2 * REQS) + (row >> 4) * 2
    source = recent[...]
    for j in range(2):
        choice = jnp.where((col == home + j) & ((row & 15) < STEPS), 1.0, 0.0).astype(BF16)
        fresh[j] = jnp.dot(choice, source, preferred_element_type=F32).astype(BF16)

    at = lax.broadcasted_iota(jnp.int32, (ROWS, REQS), 0)
    req = lax.broadcasted_iota(jnp.int32, (ROWS, REQS), 1)
    base = jnp.sum(
        jnp.where((at & (REQS - 1)) == req, len_row[...].astype(F32), 0.0), axis=1, keepdims=True
    )
    step = (lax.broadcasted_iota(jnp.int32, (ROWS, 1), 0) >> 5).astype(F32)
    angles = (base + step) * freq[...]
    cos = jnp.cos(angles)
    sin = jnp.sin(angles)
    lane = lax.broadcasted_iota(jnp.int32, (ROWS, HD), 1)
    sin = jnp.where(lane < HD // 2, -sin, sin)

    for k in range(chunks):
        for copy in load(k):
            copy.wait()
        if k == 2:
            kv_copy.start()
        if k >= 4:
            for i in (2 * k - 8, 2 * k - 7):
                weight(i).start()
        cut = pl.ds(k * depth, depth)
        part = jnp.dot(x[:, cut], q_w[cut], preferred_element_type=F32)
        if k == 0:
            acc[...] = part
        else:
            acc[...] += part

    for g in range(GROUP):
        head = acc[:, g * HD:(g + 1) * HD]
        turned[g * ROWS:(g + 1) * ROWS] = head * cos + pltpu.roll(head, HD // 2, 1) * sin

    kv_copy.wait()
    scale = HD ** -0.5
    spot = lax.broadcasted_iota(jnp.int32, (16, WIDE), 1)
    when = lax.broadcasted_iota(jnp.int32, (16, WIDE), 0) & (STEPS - 1)
    causal = (spot >= SPAN) & (spot - SPAN <= when)
    rest = jnp.zeros((WIDE - SPAN - 16, HD), BF16)

    def pages(r, j):
        cached = [kv[table[p, r], j] for p in range(MAXP)]
        return jnp.concatenate(cached + [fresh[j, r * 16:(r + 1) * 16], rest], axis=0)

    for r in range(REQS):
        query = turned[pl.ds(r, 16, stride=REQS), :].astype(BF16)
        found = lax.dot_general(
            query, pages(r, 0), (((1,), (1,)), ((), ())), preferred_element_type=F32
        ) * scale
        live = (spot < lengths[r]) | causal
        scores[r * 16:(r + 1) * 16] = jnp.where(live, found, -1e30)

    held = scores[...]
    top = jnp.max(held, axis=1, keepdims=True)
    raised = jnp.exp(held - top)
    total = jnp.sum(raised, axis=1, keepdims=True)
    probs[...] = (raised * (1.0 / total)).astype(BF16)

    for r in range(REQS):
        mixed[pl.ds(r, 16, stride=REQS), :] = jnp.dot(
            probs[r * 16:(r + 1) * 16], pages(r, 1), preferred_element_type=F32
        )

    rows = jnp.concatenate(
        [mixed[g * ROWS:(g + 1) * ROWS].astype(BF16) for g in range(GROUP)], axis=1
    )
    for i in range(len(order)):
        weight(i).wait()
        into[i][...] = jnp.dot(rows, o_w[i], preferred_element_type=F32).astype(BF16)


def relay_kernel(up1, down0, far1, far0, next_up, next_down):
    next_up[...] = (up1[...].astype(F32) + far1[...].astype(F32)).astype(BF16)
    next_down[...] = (down0[...].astype(F32) + far0[...].astype(F32)).astype(BF16)


def sum_kernel(own, up1, down1, out):
    out[...] = (own[1].astype(F32) + up1[...].astype(F32) + down1[...].astype(F32)).astype(BF16)


def close_kernel(own, up0, down0, other, pick, home, slots):
    total = (
        own[0].astype(F32) + up0[...].astype(F32) + down0[...].astype(F32) + other[...].astype(F32)
    ).astype(BF16)
    both = jnp.dot(pick[...], total, preferred_element_type=F32).astype(BF16)
    home[...] = both[:ROWS]
    slots[...] = both[ROWS:]


def arrive_kernel(rows, out):
    to = lax.broadcasted_iota(jnp.int32, (ROWS, ROWS), 0)
    come = lax.broadcasted_iota(jnp.int32, (ROWS, ROWS), 1)
    t, s, c = to >> 5, (to >> 1) & (INST - 1), to & (CAP - 1)
    turn = jnp.where(come == s * (STEPS * CAP) + t * CAP + c, 1.0, 0.0).astype(BF16)
    out[...] = jnp.dot(turn, rows[...], preferred_element_type=F32).astype(BF16)


def copy_kernel(got, out):
    out[...] = got[...]


def local(
    hidden, query_weight, output_weight, kv_pool, new_kv,
    lengths, page_table, mig_req, mig_dest, resume,
):
    width = hidden.shape[-1]
    share = width // lax.axis_size("tp")
    table = page_table.T
    hbm = functools.partial(pltpu.with_memory_space_constraint, memory_space=pltpu.HBM)
    send, pick = pl.pallas_call(
        pack_kernel,
        out_shape=(
            pltpu.HBM((INST * CAP, MAXP) + kv_pool.shape[1:], BF16),
            jax.ShapeDtypeStruct((2 * ROWS, ROWS), BF16),
        ),
        in_specs=[ANY] * 5,
        out_specs=(ANY, VMEM),
        scratch_shapes=[
            pltpu.SMEM((MAXP, REQS), jnp.int32),
            pltpu.SMEM((MIG,), jnp.int32),
            pltpu.SMEM((MIG,), jnp.int32),
            pltpu.SMEM((MIG,), jnp.int32),
            pltpu.SMEM((INST * CAP,), jnp.int32),
            pltpu.SMEM((INST,), jnp.int32),
            pltpu.VMEM(kv_pool.shape, BF16),
            pltpu.VMEM((MAXP,) + kv_pool.shape[1:], BF16),
            pltpu.VMEM((2 * ROWS, ROWS), F32),
            pltpu.SemaphoreType.DMA,
            pltpu.SemaphoreType.DMA,
            pltpu.SemaphoreType.DMA((4,)),
        ],
        compiler_params=pltpu.CompilerParams(vmem_limit_bytes=FULL_VMEM),
        cost_estimate=pl.CostEstimate(flops=0, bytes_accessed=6 << 20, transcendentals=0),
        name="pack_pages",
    )(hbm(table), hbm(mig_req), hbm(mig_dest.reshape(-1)), hbm(resume), hbm(kv_pool))
    arrival_cache = lax.all_to_all(send, "inst", split_axis=0, concat_axis=0, tiled=True)

    half = HD // 2
    inverse = np.float32(ROPE_BASE) ** (-np.arange(half, dtype=np.float32) * np.float32(2.0) / np.float32(HD))
    freq = jnp.asarray(np.concatenate([inverse, inverse])[None, :].astype(np.float32))
    chunks = 8
    piece = jax.ShapeDtypeStruct((ROWS, share), BF16)
    far1, far0, up0, down1, up1, down0, own = pl.pallas_call(
        attend_kernel,
        out_shape=(pltpu.VMEM((ROWS, share), BF16),) * 6 + (pltpu.VMEM((2, ROWS, share), BF16),),
        in_specs=[ANY] * 9,
        out_specs=(VMEM,) * 7,
        scratch_shapes=[
            pltpu.VMEM((ROWS, width), BF16),
            pltpu.VMEM(query_weight.shape, BF16),
            pltpu.VMEM((2 * RING, GROUP * HD, share), BF16),
            pltpu.VMEM(kv_pool.shape, BF16),
            pltpu.VMEM((2, REQS * 16, HD), BF16),
            pltpu.VMEM((GROUP * ROWS, HD), F32),
            pltpu.VMEM((REQS * 16, WIDE), F32),
            pltpu.VMEM((REQS * 16, WIDE), BF16),
            pltpu.VMEM((GROUP * ROWS, HD), F32),
            pltpu.VMEM((ROWS, GROUP * HD), F32),
            pltpu.VMEM((2 * ROWS, HD), BF16),
            pltpu.SMEM((REQS,), jnp.int32),
            pltpu.SMEM((MAXP, REQS), jnp.int32),
            pltpu.VMEM((1, REQS), jnp.int32),
            pltpu.VMEM((1, HD), F32),
            pltpu.SemaphoreType.DMA((chunks,)),
            pltpu.SemaphoreType.DMA((chunks,)),
            pltpu.SemaphoreType.DMA((2 * RING,)),
            pltpu.SemaphoreType.DMA,
            pltpu.SemaphoreType.DMA((5,)),
        ],
        compiler_params=pltpu.CompilerParams(vmem_limit_bytes=FULL_VMEM),
        cost_estimate=pl.CostEstimate(flops=2_400_000_000, bytes_accessed=24 << 20, transcendentals=200_000),
        name="attend",
    )(
        hbm(hidden.reshape(ROWS, width)), hbm(query_weight), hbm(output_weight), hbm(kv_pool),
        hbm(new_kv.reshape(2 * ROWS, HD)), hbm(lengths), hbm(table), hbm(lengths.reshape(1, REQS)), hbm(freq),
    )

    def shift(k):
        return [(s, (s // RING) * RING + (s + k) % RING) for s in range(2 * RING)]

    def small(kernel, out, name):
        return pl.pallas_call(
            kernel,
            out_shape=out,
            compiler_params=pltpu.CompilerParams(vmem_limit_bytes=SMALL_VMEM),
            cost_estimate=pl.CostEstimate(flops=0, bytes_accessed=2 << 20, transcendentals=0),
            name=name,
        )

    far1 = lax.ppermute(far1, "tp", shift(1))
    far0 = lax.ppermute(far0, "tp", shift(-1))
    up0 = lax.ppermute(up0, "tp", shift(1))
    down1 = lax.ppermute(down1, "tp", shift(-1))
    next_up, next_down = small(relay_kernel, (piece,) * 2, "relay")(up1, down0, far1, far0)
    up1 = lax.ppermute(next_up, "tp", shift(1))
    down0 = lax.ppermute(next_down, "tp", shift(-1))
    part = small(sum_kernel, piece, "sum_ring")(own, up1, down1)
    other = lax.ppermute(part, "tp", [(s, (s + RING) % (2 * RING)) for s in range(2 * RING)])
    home, slots = small(close_kernel, (piece, pltpu.HBM((ROWS, share), BF16)), "close")(
        own, up0, down0, other, pick
    )
    arrival_cache, slots = lax.optimization_barrier((arrival_cache, slots))
    rows = lax.all_to_all(
        slots.reshape(INST, STEPS * CAP, share), "inst", split_axis=0, concat_axis=0, tiled=True
    )
    arrival = small(arrive_kernel, piece, "arrive")(rows.reshape(ROWS, share))
    block = pl.BlockSpec((4,) + arrival_cache.shape[1:], lambda i: (i, 0, 0, 0, 0))
    arrival_cache = pl.pallas_call(
        copy_kernel,
        out_shape=jax.ShapeDtypeStruct(arrival_cache.shape, BF16),
        grid=(INST * CAP // 4,),
        in_specs=[block],
        out_specs=block,
        compiler_params=pltpu.CompilerParams(vmem_limit_bytes=SMALL_VMEM),
        cost_estimate=pl.CostEstimate(flops=0, bytes_accessed=6 << 20, transcendentals=0),
        name="keep_pages",
    )(arrival_cache)
    return (
        home.reshape(STEPS, REQS, share),
        arrival.reshape(STEPS, INST * CAP, share),
        arrival_cache,
    )


def solution(mesh):
    in_specs = (
        P(None, "inst", None),
        P(None, "tp"),
        P("tp", None),
        P("inst", None, None, "tp"),
        P(None, "inst", None, "tp"),
        P("inst"),
        P("inst", None),
        P("inst"),
        P("inst", None),
        P("inst"),
    )
    out_specs = (P(None, "inst", "tp"), P(None, "inst", "tp"), P("inst", None, None, None, "tp"))
    return jax.shard_map(local, mesh=mesh, in_specs=in_specs, out_specs=out_specs, check_vma=False)
```

```python
import functools

import jax
import jax.numpy as jnp
import numpy as np
from jax import lax
from jax.experimental import pallas as pl
from jax.experimental.pallas import tpu as pltpu
from jax.sharding import PartitionSpec as P

HD = 128
GROUP = 4
CAP = 2
STEPS = 4
REQS = 32
MIG = 16
INST = 16
PAGE = 64
MAXP = 3
RING = 4
SPAN = MAXP * PAGE
ROWS = STEPS * REQS
WIDE = 256
ROPE_BASE = 500000.0
FULL_VMEM = 48 << 20
SMALL_VMEM = 6 << 20
F32 = jnp.float32
BF16 = jnp.bfloat16
SMEM = pl.BlockSpec(memory_space=pltpu.SMEM)
VMEM = pl.BlockSpec(memory_space=pltpu.VMEM)
ANY = pl.BlockSpec(memory_space=pl.ANY)


def pack_kernel(
    page_list, req_list, dest_list, resume_list, pool, send, pick,
    table, mreq, mdest, resume, slot_req, count, kv, zeros, wide, kv_sem, sem, small_sem,
):
    load = pltpu.make_async_copy(pool, kv, kv_sem)
    load.start()
    small = [
        pltpu.make_async_copy(source, target, small_sem.at[i])
        for i, (source, target) in enumerate((
            (req_list, mreq), (dest_list, mdest), (resume_list, resume), (page_list, table),
        ))
    ]
    for copy in small:
        copy.start()
    zeros[...] = jnp.zeros_like(zeros)

    def clear(s, carry):
        slot_req[s] = -1
        return carry

    def fresh(d, carry):
        count[d] = 0
        return carry

    lax.fori_loop(0, INST * CAP, clear, 0)
    lax.fori_loop(0, INST, fresh, 0)

    for copy in small:
        copy.wait()

    def place(k, carry):
        d = mdest[k]
        c = count[d]
        count[d] = c + 1
        slot_req[d * CAP + c] = mreq[k]
        return carry

    lax.fori_loop(0, MIG, place, 0)
    here_at = lax.axis_index("inst")
    rows = lax.broadcasted_iota(jnp.int32, (2 * ROWS, ROWS), 0)
    cols = lax.broadcasted_iota(jnp.int32, (2 * ROWS, ROWS), 1)
    wide[...] = jnp.where(rows == cols, 1.0, 0.0).astype(F32)
    lane = lax.broadcasted_iota(jnp.int32, (1, ROWS), 1)

    def clear_count(d, carry):
        count[d] = 0
        return carry

    lax.fori_loop(0, INST, clear_count, 0)

    def choose(k, carry):
        d = mdest[k]
        c = count[d]
        count[d] = c + 1
        req = mreq[k]
        first = resume[k]
        far = (d >> 3) ^ (here_at >> 3)
        cross = (d ^ here_at) & 1
        ahead = ((d >> 1) - (here_at >> 1)) & (RING - 1)
        block = ROWS + far * (ROWS // 2) + cross * (ROWS // 4) + ahead * (STEPS * CAP)
        for t in range(STEPS):
            at = t * REQS + req
            here = jnp.where(lane == at, 1.0, 0.0).astype(F32)
            stay = jnp.where(t < first, 1.0, 0.0).astype(F32)
            wide[pl.ds(at, 1), :] = here * stay
            wide[pl.ds(block + t * CAP + c, 1), :] = here * (1.0 - stay)
        return carry

    lax.fori_loop(0, MIG, choose, 0)
    pick[...] = wide[...].astype(BF16)
    load.wait()

    def ship(s, carry):
        req = slot_req[s]

        @pl.when(req >= 0)
        def _():
            for p in range(MAXP):
                pltpu.make_async_copy(kv.at[table[p, req]], send.at[s, p], sem).start()

        @pl.when(req < 0)
        def _():
            pltpu.make_async_copy(zeros, send.at[s], sem).start()

        return carry

    lax.fori_loop(0, INST * CAP, ship, 0)

    pltpu.make_async_copy(send, send, sem).wait()


def attend_kernel(
    hidden, wq, wo, pool, new_kv, len_list, page_list, len_line, freq_line,
    far1, far0, up0, down1, up1, down0, own,
    x, q_w, o_w, kv, fresh, turned, scores, probs, mixed, acc,
    recent, lengths, table, len_row, freq,
    x_sem, q_sem, o_sem, kv_sem, small_sem,
):
    chunks = x_sem.shape[0]
    depth = x.shape[1] // chunks
    share = own.shape[-1]
    tp = lax.axis_index("tp")
    y, z = tp // RING, tp % RING

    def load(k):
        cut = pl.ds(k * depth, depth)
        return (
            pltpu.make_async_copy(hidden.at[:, cut], x.at[:, cut], x_sem.at[k]),
            pltpu.make_async_copy(wq.at[cut], q_w.at[cut], q_sem.at[k]),
        )

    small = [
        pltpu.make_async_copy(source, target, small_sem.at[i])
        for i, (source, target) in enumerate((
            (new_kv, recent), (len_line, len_row), (freq_line, freq), (len_list, lengths), (page_list, table),
        ))
    ]
    for k in range(chunks):
        for copy in load(k):
            copy.start()
        if k == 0:
            for copy in small:
                copy.start()
    kv_copy = pltpu.make_async_copy(pool, kv, kv_sem)
    order = [(2, 1), (2, 0), (1, 0), (3, 1), (1, 1), (3, 0), (0, 1), (0, 0)]
    into = (far1, far0, up0, down1, up1, down0, own.at[1], own.at[0])

    def weight(i):
        k, j = order[i]
        n = lax.rem(y + j, 2) * RING + lax.rem(z + k, RING)
        cut = pl.ds(pl.multiple_of(n * share, share), share)
        return pltpu.make_async_copy(wo.at[:, cut], o_w.at[i], o_sem.at[i])

    for copy in small:
        copy.wait()

    row = lax.broadcasted_iota(jnp.int32, (REQS * 16, ROWS * 2), 0)
    col = lax.broadcasted_iota(jnp.int32, (REQS * 16, ROWS * 2), 1)
    home = (row & 15) * (2 * REQS) + (row >> 4) * 2
    source = recent[...]
    for j in range(2):
        choice = jnp.where((col == home + j) & ((row & 15) < STEPS), 1.0, 0.0).astype(BF16)
        fresh[j] = jnp.dot(choice, source, preferred_element_type=F32).astype(BF16)

    at = lax.broadcasted_iota(jnp.int32, (ROWS, REQS), 0)
    req = lax.broadcasted_iota(jnp.int32, (ROWS, REQS), 1)
    base = jnp.sum(
        jnp.where((at & (REQS - 1)) == req, len_row[...].astype(F32), 0.0), axis=1, keepdims=True
    )
    step = (lax.broadcasted_iota(jnp.int32, (ROWS, 1), 0) >> 5).astype(F32)
    angles = (base + step) * freq[...]
    cos = jnp.cos(angles)
    sin = jnp.sin(angles)
    lane = lax.broadcasted_iota(jnp.int32, (ROWS, HD), 1)
    sin = jnp.where(lane < HD // 2, -sin, sin)

    for k in range(chunks):
        for copy in load(k):
            copy.wait()
        if k == 2:
            kv_copy.start()
        if k >= 4:
            for i in (2 * k - 8, 2 * k - 7):
                weight(i).start()
        cut = pl.ds(k * depth, depth)
        part = jnp.dot(x[:, cut], q_w[cut], preferred_element_type=F32)
        if k == 0:
            acc[...] = part
        else:
            acc[...] += part

    for g in range(GROUP):
        head = acc[:, g * HD:(g + 1) * HD]
        turned[g * ROWS:(g + 1) * ROWS] = head * cos + pltpu.roll(head, HD // 2, 1) * sin

    kv_copy.wait()
    scale = HD ** -0.5
    spot = lax.broadcasted_iota(jnp.int32, (16, WIDE), 1)
    when = lax.broadcasted_iota(jnp.int32, (16, WIDE), 0) & (STEPS - 1)
    causal = (spot >= SPAN) & (spot - SPAN <= when)
    rest = jnp.zeros((WIDE - SPAN - 16, HD), BF16)

    def pages(r, j):
        cached = [kv[table[p, r], j] for p in range(MAXP)]
        return jnp.concatenate(cached + [fresh[j, r * 16:(r + 1) * 16], rest], axis=0)

    for r in range(REQS):
        query = turned[pl.ds(r, 16, stride=REQS), :].astype(BF16)
        found = lax.dot_general(
            query, pages(r, 0), (((1,), (1,)), ((), ())), preferred_element_type=F32
        ) * scale
        live = (spot < lengths[r]) | causal
        scores[r * 16:(r + 1) * 16] = jnp.where(live, found, -1e30)

    held = scores[...]
    top = jnp.max(held, axis=1, keepdims=True)
    raised = jnp.exp(held - top)
    total = jnp.sum(raised, axis=1, keepdims=True)
    probs[...] = (raised * (1.0 / total)).astype(BF16)

    for r in range(REQS):
        mixed[pl.ds(r, 16, stride=REQS), :] = jnp.dot(
            probs[r * 16:(r + 1) * 16], pages(r, 1), preferred_element_type=F32
        )

    rows = jnp.concatenate(
        [mixed[g * ROWS:(g + 1) * ROWS].astype(BF16) for g in range(GROUP)], axis=1
    )
    for i in range(len(order)):
        weight(i).wait()
        into[i][...] = jnp.dot(rows, o_w[i], preferred_element_type=F32).astype(BF16)


def relay_kernel(up1, down0, far1, far0, next_up, next_down):
    next_up[...] = (up1[...].astype(F32) + far1[...].astype(F32)).astype(BF16)
    next_down[...] = (down0[...].astype(F32) + far0[...].astype(F32)).astype(BF16)


def close_kernel(
    own, up0, up1, down0, down1, pick, keep, pass_on, near0, near1, far0, far1
):
    choice = pick[ROWS:]
    mine = (own[0].astype(F32) + up0[...].astype(F32) + down0[...].astype(F32)).astype(BF16)
    other = (own[1].astype(F32) + up1[...].astype(F32) + down1[...].astype(F32)).astype(BF16)
    keep[...] = mine
    pass_on[...] = other
    for part, near, far in ((mine, near0, far0), (other, near1, far1)):
        taken = jnp.dot(choice, part, preferred_element_type=F32).astype(BF16)
        near[...] = taken[:ROWS // 2]
        far[...] = taken[ROWS // 2:]


def home_kernel(keep, other, pick, home):
    total = (keep[...].astype(F32) + other[...].astype(F32)).astype(BF16)
    home[...] = jnp.dot(pick[:ROWS], total, preferred_element_type=F32).astype(BF16)


def join_kernel(near0, near1, far0, far1, kept, same, cross):
    near = (near0[...].astype(F32) + near1[...].astype(F32)).astype(BF16)
    far = (far0[...].astype(F32) + far1[...].astype(F32)).astype(BF16)
    to = lax.broadcasted_iota(jnp.int32, (ROWS, ROWS), 0)
    come = lax.broadcasted_iota(jnp.int32, (ROWS, ROWS), 1)
    source = ((to >> 3) & 1) * (ROWS // 2) + (to >> 4) * (STEPS * CAP) + (to & 7)
    turn = jnp.where(come == source, 1.0, 0.0).astype(BF16)
    rows = jnp.dot(turn, jnp.concatenate([near, far], axis=0), preferred_element_type=F32).astype(BF16)
    same[...] = rows[:ROWS // 2]
    cross[...] = rows[ROWS // 2:]


def split_kernel(same, crossed, *ahead):
    for k in range(RING):
        ahead[k][:16] = same[k * 16:(k + 1) * 16]
        ahead[k][16:] = crossed[k * 16:(k + 1) * 16]


def arrive_kernel(k0, k1, k2, k3, out):
    here_at = lax.axis_index("inst")
    rows = jnp.concatenate([k0[...], k1[...], k2[...], k3[...]], axis=0)
    to = lax.broadcasted_iota(jnp.int32, (ROWS, ROWS), 0)
    come = lax.broadcasted_iota(jnp.int32, (ROWS, ROWS), 1)
    t, s, c = to >> 5, (to >> 1) & (INST - 1), to & (CAP - 1)
    behind = ((here_at >> 1) - (s >> 1)) & (RING - 1)
    cross = (s ^ here_at) & 1
    far = ((s ^ here_at) >> 3) & 1
    source = behind * 32 + cross * 16 + far * 8 + t * CAP + c
    turn = jnp.where(come == source, 1.0, 0.0).astype(BF16)
    out[...] = jnp.dot(turn, rows, preferred_element_type=F32).astype(BF16)


def copy_kernel(got, out):
    out[...] = got[...]


def local(
    hidden, query_weight, output_weight, kv_pool, new_kv,
    lengths, page_table, mig_req, mig_dest, resume,
):
    width = hidden.shape[-1]
    share = width // lax.axis_size("tp")
    table = page_table.T
    hbm = functools.partial(pltpu.with_memory_space_constraint, memory_space=pltpu.HBM)
    send, pick = pl.pallas_call(
        pack_kernel,
        out_shape=(
            pltpu.HBM((INST * CAP, MAXP) + kv_pool.shape[1:], BF16),
            jax.ShapeDtypeStruct((2 * ROWS, ROWS), BF16),
        ),
        in_specs=[ANY] * 5,
        out_specs=(ANY, VMEM),
        scratch_shapes=[
            pltpu.SMEM((MAXP, REQS), jnp.int32),
            pltpu.SMEM((MIG,), jnp.int32),
            pltpu.SMEM((MIG,), jnp.int32),
            pltpu.SMEM((MIG,), jnp.int32),
            pltpu.SMEM((INST * CAP,), jnp.int32),
            pltpu.SMEM((INST,), jnp.int32),
            pltpu.VMEM(kv_pool.shape, BF16),
            pltpu.VMEM((MAXP,) + kv_pool.shape[1:], BF16),
            pltpu.VMEM((2 * ROWS, ROWS), F32),
            pltpu.SemaphoreType.DMA,
            pltpu.SemaphoreType.DMA,
            pltpu.SemaphoreType.DMA((4,)),
        ],
        compiler_params=pltpu.CompilerParams(vmem_limit_bytes=FULL_VMEM),
        cost_estimate=pl.CostEstimate(flops=0, bytes_accessed=6 << 20, transcendentals=0),
        name="pack_pages",
    )(hbm(table), hbm(mig_req), hbm(mig_dest.reshape(-1)), hbm(resume), hbm(kv_pool))
    arrival_cache = lax.all_to_all(send, "inst", split_axis=0, concat_axis=0, tiled=True)

    half = HD // 2
    inverse = np.float32(ROPE_BASE) ** (-np.arange(half, dtype=np.float32) * np.float32(2.0) / np.float32(HD))
    freq = jnp.asarray(np.concatenate([inverse, inverse])[None, :].astype(np.float32))
    chunks = 8
    piece = jax.ShapeDtypeStruct((ROWS, share), BF16)
    far1, far0, up0, down1, up1, down0, own = pl.pallas_call(
        attend_kernel,
        out_shape=(pltpu.VMEM((ROWS, share), BF16),) * 6 + (pltpu.VMEM((2, ROWS, share), BF16),),
        in_specs=[ANY] * 9,
        out_specs=(VMEM,) * 7,
        scratch_shapes=[
            pltpu.VMEM((ROWS, width), BF16),
            pltpu.VMEM(query_weight.shape, BF16),
            pltpu.VMEM((2 * RING, GROUP * HD, share), BF16),
            pltpu.VMEM(kv_pool.shape, BF16),
            pltpu.VMEM((2, REQS * 16, HD), BF16),
            pltpu.VMEM((GROUP * ROWS, HD), F32),
            pltpu.VMEM((REQS * 16, WIDE), F32),
            pltpu.VMEM((REQS * 16, WIDE), BF16),
            pltpu.VMEM((GROUP * ROWS, HD), F32),
            pltpu.VMEM((ROWS, GROUP * HD), F32),
            pltpu.VMEM((2 * ROWS, HD), BF16),
            pltpu.SMEM((REQS,), jnp.int32),
            pltpu.SMEM((MAXP, REQS), jnp.int32),
            pltpu.VMEM((1, REQS), jnp.int32),
            pltpu.VMEM((1, HD), F32),
            pltpu.SemaphoreType.DMA((chunks,)),
            pltpu.SemaphoreType.DMA((chunks,)),
            pltpu.SemaphoreType.DMA((2 * RING,)),
            pltpu.SemaphoreType.DMA,
            pltpu.SemaphoreType.DMA((5,)),
        ],
        compiler_params=pltpu.CompilerParams(vmem_limit_bytes=FULL_VMEM),
        cost_estimate=pl.CostEstimate(flops=2_400_000_000, bytes_accessed=24 << 20, transcendentals=200_000),
        name="attend",
    )(
        hbm(hidden.reshape(ROWS, width)), hbm(query_weight), hbm(output_weight), hbm(kv_pool),
        hbm(new_kv.reshape(2 * ROWS, HD)), hbm(lengths), hbm(table), hbm(lengths.reshape(1, REQS)), hbm(freq),
    )

    def shift(k):
        return [(s, (s // RING) * RING + (s + k) % RING) for s in range(2 * RING)]

    def small(kernel, out, name, **specs):
        return pl.pallas_call(
            kernel,
            out_shape=out,
            **specs,
            compiler_params=pltpu.CompilerParams(vmem_limit_bytes=SMALL_VMEM),
            cost_estimate=pl.CostEstimate(flops=0, bytes_accessed=2 << 20, transcendentals=0),
            name=name,
        )

    far1 = lax.ppermute(far1, "tp", shift(1))
    far0 = lax.ppermute(far0, "tp", shift(-1))
    up0 = lax.ppermute(up0, "tp", shift(1))
    down1 = lax.ppermute(down1, "tp", shift(-1))
    next_up, next_down = small(relay_kernel, (piece,) * 2, "relay")(up1, down0, far1, far0)
    up1 = lax.ppermute(next_up, "tp", shift(1))
    down0 = lax.ppermute(next_down, "tp", shift(-1))
    half_piece = jax.ShapeDtypeStruct((ROWS // 2, share), BF16)
    keep, pass_on, near0, near1, far0, far1 = small(
        close_kernel, (piece,) * 2 + (half_piece,) * 4, "close"
    )(own, up0, up1, down0, down1, pick)
    flip_y = [(s, (s + RING) % (2 * RING)) for s in range(2 * RING)]
    flip_far = [(s, s ^ 8) for s in range(INST)]
    both = [
        (i * 2 * RING + s, (i ^ 8) * 2 * RING + (s + RING) % (2 * RING))
        for i in range(INST) for s in range(2 * RING)
    ]
    far0 = lax.ppermute(far0, "inst", flip_far)
    near1 = lax.ppermute(near1, "tp", flip_y)
    far1 = lax.ppermute(far1, ("inst", "tp"), both)
    block = pl.BlockSpec((4,) + arrival_cache.shape[1:], lambda i: (i, 0, 0, 0, 0))
    arrival_cache = pl.pallas_call(
        copy_kernel,
        out_shape=jax.ShapeDtypeStruct(arrival_cache.shape, BF16),
        grid=(INST * CAP // 4,),
        in_specs=[block],
        out_specs=block,
        compiler_params=pltpu.CompilerParams(vmem_limit_bytes=SMALL_VMEM),
        cost_estimate=pl.CostEstimate(flops=0, bytes_accessed=6 << 20, transcendentals=0),
        name="keep_pages",
    )(arrival_cache)
    same, cross = small(join_kernel, (half_piece,) * 2, "join", in_specs=[VMEM] * 4 + [ANY])(near0, near1, far0, far1, hbm(arrival_cache))
    other = lax.ppermute(pass_on, "tp", flip_y)
    crossed = lax.ppermute(cross, "inst", [(s, s ^ 1) for s in range(INST)])
    ahead = small(
        split_kernel, (jax.ShapeDtypeStruct((ROWS // RING, share), BF16),) * RING, "split"
    )(same, crossed)

    def along(k):
        return [(s, (s & 9) + (((s >> 1) + k) & (RING - 1)) * 2) for s in range(INST)]

    ahead = [ahead[0]] + [lax.ppermute(ahead[k], "inst", along(k)) for k in range(1, RING)]
    home = small(home_kernel, piece, "home")(keep, other, pick)
    arrival = small(arrive_kernel, piece, "arrive")(*ahead)
    return (
        home.reshape(STEPS, REQS, share),
        arrival.reshape(STEPS, INST * CAP, share),
        arrival_cache,
    )


def solution(mesh):
    in_specs = (
        P(None, "inst", None),
        P(None, "tp"),
        P("tp", None),
        P("inst", None, None, "tp"),
        P(None, "inst", None, "tp"),
        P("inst"),
        P("inst", None),
        P("inst"),
        P("inst", None),
        P("inst"),
    )
    out_specs = (P(None, "inst", "tp"), P(None, "inst", "tp"), P("inst", None, None, None, "tp"))
    return jax.shard_map(local, mesh=mesh, in_specs=in_specs, out_specs=out_specs, check_vma=False)
```

```python
import functools

import jax
import jax.numpy as jnp
import numpy as np
from jax import lax
from jax.experimental import pallas as pl
from jax.experimental.pallas import tpu as pltpu
from jax.sharding import PartitionSpec as P

HD = 128
GROUP = 4
CAP = 2
STEPS = 4
REQS = 32
MIG = 16
INST = 16
PAGE = 64
MAXP = 3
RING = 4
SPAN = MAXP * PAGE
ROWS = STEPS * REQS
WIDE = 256
LANES = 8
ROPE_BASE = 500000.0
FULL_VMEM = 48 << 20
SMALL_VMEM = 6 << 20
F32 = jnp.float32
BF16 = jnp.bfloat16
SMEM = pl.BlockSpec(memory_space=pltpu.SMEM)
VMEM = pl.BlockSpec(memory_space=pltpu.VMEM)
ANY = pl.BlockSpec(memory_space=pl.ANY)


def pack_kernel(
    page_list, req_list, dest_list, resume_list, pool, send, pick,
    table, mreq, mdest, resume, slot_of, filled, count, kv, zeros, wide, kv_sem, sem, small_sem,
):
    size = pool.shape[0] // LANES
    load = [
        pltpu.make_async_copy(pool.at[pl.ds(i * size, size)], kv.at[pl.ds(i * size, size)], kv_sem.at[i])
        for i in range(LANES)
    ]
    small = [
        pltpu.make_async_copy(source, target, small_sem.at[i])
        for i, (source, target) in enumerate((
            (req_list, mreq), (dest_list, mdest), (resume_list, resume), (page_list, table),
        ))
    ]
    for copy in small:
        copy.start()
    for copy in load:
        copy.start()
    zeros[...] = jnp.zeros_like(zeros)
    for s in range(INST * CAP):
        filled[s] = 0
    for d in range(INST):
        count[d] = 0
    for copy in small:
        copy.wait()
    for k in range(MIG):
        d = mdest[k]
        c = count[d]
        count[d] = c + 1
        slot_of[k] = d * CAP + c
        filled[d * CAP + c] = 1

    def clear(s, carry):
        @pl.when(filled[s] == 0)
        def _():
            pltpu.make_async_copy(zeros, send.at[s], sem).start()

        return carry

    lax.fori_loop(0, INST * CAP, clear, 0)
    for copy in load:
        copy.wait()
    for k in range(MIG):
        for p in range(MAXP):
            pltpu.make_async_copy(kv.at[table[p, mreq[k]]], send.at[slot_of[k], p], sem).start()

    here_at = lax.axis_index("inst")
    rows = lax.broadcasted_iota(jnp.int32, (2 * ROWS, ROWS), 0)
    cols = lax.broadcasted_iota(jnp.int32, (2 * ROWS, ROWS), 1)
    wide[...] = jnp.where(rows == cols, 1.0, 0.0).astype(F32)
    lane = lax.broadcasted_iota(jnp.int32, (1, ROWS), 1)
    for k in range(MIG):
        slot = slot_of[k]
        d, c = slot >> 1, slot & 1
        req = mreq[k]
        first = resume[k]
        far = (d >> 3) ^ (here_at >> 3)
        cross = (d ^ here_at) & 1
        ahead = ((d >> 1) - (here_at >> 1)) & (RING - 1)
        block = ROWS + far * (ROWS // 2) + cross * (ROWS // 4) + ahead * (STEPS * CAP)
        for t in range(STEPS):
            at = t * REQS + req
            wide[pl.ds(at, 1), :] = jnp.where((lane == at) & (t < first), 1.0, 0.0).astype(F32)
            wide[pl.ds(block + t * CAP + c, 1), :] = jnp.where((lane == at) & (t >= first), 1.0, 0.0).astype(F32)
    pick[...] = wide[...].astype(BF16)
    pltpu.make_async_copy(send, send, sem).wait()


def attend_kernel(
    hidden, wq, wo, pool, new_kv, len_list, page_list, len_line, freq_line,
    far1, far0, up0, down1, up1, down0, own,
    x, q_w, o_w, kv, fresh, turned, scores, probs, mixed, acc,
    recent, lengths, table, len_row, freq,
    x_sem, q_sem, o_sem, kv_sem, small_sem,
):
    chunks = x_sem.shape[0]
    depth = x.shape[1] // chunks
    share = own.shape[-1]
    tp = lax.axis_index("tp")
    y, z = tp // RING, tp % RING

    def load(k):
        cut = pl.ds(k * depth, depth)
        return (
            pltpu.make_async_copy(hidden.at[:, cut], x.at[:, cut], x_sem.at[k]),
            pltpu.make_async_copy(wq.at[cut], q_w.at[cut], q_sem.at[k]),
        )

    small = [
        pltpu.make_async_copy(source, target, small_sem.at[i])
        for i, (source, target) in enumerate((
            (new_kv, recent), (len_line, len_row), (freq_line, freq), (len_list, lengths), (page_list, table),
        ))
    ]
    for k in range(chunks):
        for copy in load(k):
            copy.start()
        if k == 0:
            for copy in small:
                copy.start()
    kv_copy = pltpu.make_async_copy(pool, kv, kv_sem)
    order = [(2, 1), (2, 0), (1, 0), (3, 1), (1, 1), (3, 0), (0, 1), (0, 0)]
    into = (far1, far0, up0, down1, up1, down0, own.at[1], own.at[0])

    def weight(i):
        k, j = order[i]
        n = lax.rem(y + j, 2) * RING + lax.rem(z + k, RING)
        cut = pl.ds(pl.multiple_of(n * share, share), share)
        return pltpu.make_async_copy(wo.at[:, cut], o_w.at[i], o_sem.at[i])

    for copy in small:
        copy.wait()

    row = lax.broadcasted_iota(jnp.int32, (REQS * 16, ROWS * 2), 0)
    col = lax.broadcasted_iota(jnp.int32, (REQS * 16, ROWS * 2), 1)
    home = (row & 15) * (2 * REQS) + (row >> 4) * 2
    source = recent[...]
    for j in range(2):
        choice = jnp.where((col == home + j) & ((row & 15) < STEPS), 1.0, 0.0).astype(BF16)
        fresh[j] = jnp.dot(choice, source, preferred_element_type=F32).astype(BF16)

    at = lax.broadcasted_iota(jnp.int32, (ROWS, REQS), 0)
    req = lax.broadcasted_iota(jnp.int32, (ROWS, REQS), 1)
    base = jnp.sum(
        jnp.where((at & (REQS - 1)) == req, len_row[...].astype(F32), 0.0), axis=1, keepdims=True
    )
    step = (lax.broadcasted_iota(jnp.int32, (ROWS, 1), 0) >> 5).astype(F32)
    angles = (base + step) * freq[...]
    cos = jnp.cos(angles)
    sin = jnp.sin(angles)
    lane = lax.broadcasted_iota(jnp.int32, (ROWS, HD), 1)
    sin = jnp.where(lane < HD // 2, -sin, sin)

    for k in range(chunks):
        for copy in load(k):
            copy.wait()
        if k == 2:
            kv_copy.start()
        if k >= 4:
            for i in (2 * k - 8, 2 * k - 7):
                weight(i).start()
        cut = pl.ds(k * depth, depth)
        part = jnp.dot(x[:, cut], q_w[cut], preferred_element_type=F32)
        if k == 0:
            acc[...] = part
        else:
            acc[...] += part

    for g in range(GROUP):
        head = acc[:, g * HD:(g + 1) * HD]
        turned[g * ROWS:(g + 1) * ROWS] = head * cos + pltpu.roll(head, HD // 2, 1) * sin

    kv_copy.wait()
    scale = HD ** -0.5
    spot = lax.broadcasted_iota(jnp.int32, (16, WIDE), 1)
    when = lax.broadcasted_iota(jnp.int32, (16, WIDE), 0) & (STEPS - 1)
    causal = (spot >= SPAN) & (spot - SPAN <= when)
    rest = jnp.zeros((WIDE - SPAN - 16, HD), BF16)

    def pages(r, j):
        cached = [kv[table[p, r], j] for p in range(MAXP)]
        return jnp.concatenate(cached + [fresh[j, r * 16:(r + 1) * 16], rest], axis=0)

    for r in range(REQS):
        query = turned[pl.ds(r, 16, stride=REQS), :].astype(BF16)
        found = lax.dot_general(
            query, pages(r, 0), (((1,), (1,)), ((), ())), preferred_element_type=F32
        ) * scale
        live = (spot < lengths[r]) | causal
        scores[r * 16:(r + 1) * 16] = jnp.where(live, found, -1e30)

    held = scores[...]
    top = jnp.max(held, axis=1, keepdims=True)
    raised = jnp.exp(held - top)
    total = jnp.sum(raised, axis=1, keepdims=True)
    probs[...] = (raised * (1.0 / total)).astype(BF16)

    for r in range(REQS):
        mixed[pl.ds(r, 16, stride=REQS), :] = jnp.dot(
            probs[r * 16:(r + 1) * 16], pages(r, 1), preferred_element_type=F32
        )

    rows = jnp.concatenate(
        [mixed[g * ROWS:(g + 1) * ROWS].astype(BF16) for g in range(GROUP)], axis=1
    )
    for i in range(len(order)):
        weight(i).wait()
        into[i][...] = jnp.dot(rows, o_w[i], preferred_element_type=F32).astype(BF16)


def relay_kernel(up1, down0, far1, far0, next_up, next_down):
    next_up[...] = (up1[...].astype(F32) + far1[...].astype(F32)).astype(BF16)
    next_down[...] = (down0[...].astype(F32) + far0[...].astype(F32)).astype(BF16)


def close_kernel(
    own, up0, up1, down0, down1, pick, keep, pass_on, near0, near1, far0, far1
):
    choice = pick[ROWS:]
    mine = (own[0].astype(F32) + up0[...].astype(F32) + down0[...].astype(F32)).astype(BF16)
    other = (own[1].astype(F32) + up1[...].astype(F32) + down1[...].astype(F32)).astype(BF16)
    keep[...] = mine
    pass_on[...] = other
    for part, near, far in ((mine, near0, far0), (other, near1, far1)):
        taken = jnp.dot(choice, part, preferred_element_type=F32).astype(BF16)
        near[...] = taken[:ROWS // 2]
        far[...] = taken[ROWS // 2:]


def home_kernel(keep, other, pick, home):
    total = (keep[...].astype(F32) + other[...].astype(F32)).astype(BF16)
    home[...] = jnp.dot(pick[:ROWS], total, preferred_element_type=F32).astype(BF16)


def join_kernel(near0, near1, far0, far1, same, cross):
    near = (near0[...].astype(F32) + near1[...].astype(F32)).astype(BF16)
    far = (far0[...].astype(F32) + far1[...].astype(F32)).astype(BF16)
    to = lax.broadcasted_iota(jnp.int32, (ROWS, ROWS), 0)
    come = lax.broadcasted_iota(jnp.int32, (ROWS, ROWS), 1)
    source = ((to >> 3) & 1) * (ROWS // 2) + (to >> 4) * (STEPS * CAP) + (to & 7)
    turn = jnp.where(come == source, 1.0, 0.0).astype(BF16)
    rows = jnp.dot(turn, jnp.concatenate([near, far], axis=0), preferred_element_type=F32).astype(BF16)
    same[...] = rows[:ROWS // 2]
    cross[...] = rows[ROWS // 2:]


def split_kernel(same, crossed, *ahead):
    for k in range(RING):
        ahead[k][:16] = same[k * 16:(k + 1) * 16]
        ahead[k][16:] = crossed[k * 16:(k + 1) * 16]


def arrive_kernel(k0, k1, k2, k3, kept, out):
    here_at = lax.axis_index("inst")
    rows = jnp.concatenate([k0[...], k1[...], k2[...], k3[...]], axis=0)
    to = lax.broadcasted_iota(jnp.int32, (ROWS, ROWS), 0)
    come = lax.broadcasted_iota(jnp.int32, (ROWS, ROWS), 1)
    t, s, c = to >> 5, (to >> 1) & (INST - 1), to & (CAP - 1)
    behind = ((here_at >> 1) - (s >> 1)) & (RING - 1)
    cross = (s ^ here_at) & 1
    far = ((s ^ here_at) >> 3) & 1
    source = behind * 32 + cross * 16 + far * 8 + t * CAP + c
    turn = jnp.where(come == source, 1.0, 0.0).astype(BF16)
    out[...] = jnp.dot(turn, rows, preferred_element_type=F32).astype(BF16)


def keep_kernel(got, after, out, sem):
    size = got.shape[0] // LANES
    copies = [
        pltpu.make_async_copy(got.at[pl.ds(i * size, size)], out.at[pl.ds(i * size, size)], sem.at[i])
        for i in range(LANES)
    ]
    for copy in copies:
        copy.start()
    for copy in copies:
        copy.wait()


def local(
    hidden, query_weight, output_weight, kv_pool, new_kv,
    lengths, page_table, mig_req, mig_dest, resume,
):
    width = hidden.shape[-1]
    share = width // lax.axis_size("tp")
    table = page_table.T
    hbm = functools.partial(pltpu.with_memory_space_constraint, memory_space=pltpu.HBM)
    send, pick = pl.pallas_call(
        pack_kernel,
        out_shape=(
            pltpu.HBM((INST * CAP, MAXP) + kv_pool.shape[1:], BF16),
            jax.ShapeDtypeStruct((2 * ROWS, ROWS), BF16),
        ),
        in_specs=[ANY] * 5,
        out_specs=(ANY, VMEM),
        scratch_shapes=[
            pltpu.SMEM((MAXP, REQS), jnp.int32),
            pltpu.SMEM((MIG,), jnp.int32),
            pltpu.SMEM((MIG,), jnp.int32),
            pltpu.SMEM((MIG,), jnp.int32),
            pltpu.SMEM((MIG,), jnp.int32),
            pltpu.SMEM((INST * CAP,), jnp.int32),
            pltpu.SMEM((INST,), jnp.int32),
            pltpu.VMEM(kv_pool.shape, BF16),
            pltpu.VMEM((MAXP,) + kv_pool.shape[1:], BF16),
            pltpu.VMEM((2 * ROWS, ROWS), F32),
            pltpu.SemaphoreType.DMA((LANES,)),
            pltpu.SemaphoreType.DMA,
            pltpu.SemaphoreType.DMA((4,)),
        ],
        compiler_params=pltpu.CompilerParams(vmem_limit_bytes=FULL_VMEM),
        cost_estimate=pl.CostEstimate(flops=0, bytes_accessed=6 << 20, transcendentals=0),
        name="pack_pages",
    )(hbm(table), hbm(mig_req), hbm(mig_dest.reshape(-1)), hbm(resume), hbm(kv_pool))
    arrival_cache = lax.all_to_all(send, "inst", split_axis=0, concat_axis=0, tiled=True)

    half = HD // 2
    inverse = np.float32(ROPE_BASE) ** (-np.arange(half, dtype=np.float32) * np.float32(2.0) / np.float32(HD))
    freq = jnp.asarray(np.concatenate([inverse, inverse])[None, :].astype(np.float32))
    chunks = 8
    piece = jax.ShapeDtypeStruct((ROWS, share), BF16)
    far1, far0, up0, down1, up1, down0, own = pl.pallas_call(
        attend_kernel,
        out_shape=(pltpu.VMEM((ROWS, share), BF16),) * 6 + (pltpu.VMEM((2, ROWS, share), BF16),),
        in_specs=[ANY] * 9,
        out_specs=(VMEM,) * 7,
        scratch_shapes=[
            pltpu.VMEM((ROWS, width), BF16),
            pltpu.VMEM(query_weight.shape, BF16),
            pltpu.VMEM((2 * RING, GROUP * HD, share), BF16),
            pltpu.VMEM(kv_pool.shape, BF16),
            pltpu.VMEM((2, REQS * 16, HD), BF16),
            pltpu.VMEM((GROUP * ROWS, HD), F32),
            pltpu.VMEM((REQS * 16, WIDE), F32),
            pltpu.VMEM((REQS * 16, WIDE), BF16),
            pltpu.VMEM((GROUP * ROWS, HD), F32),
            pltpu.VMEM((ROWS, GROUP * HD), F32),
            pltpu.VMEM((2 * ROWS, HD), BF16),
            pltpu.SMEM((REQS,), jnp.int32),
            pltpu.SMEM((MAXP, REQS), jnp.int32),
            pltpu.VMEM((1, REQS), jnp.int32),
            pltpu.VMEM((1, HD), F32),
            pltpu.SemaphoreType.DMA((chunks,)),
            pltpu.SemaphoreType.DMA((chunks,)),
            pltpu.SemaphoreType.DMA((2 * RING,)),
            pltpu.SemaphoreType.DMA,
            pltpu.SemaphoreType.DMA((5,)),
        ],
        compiler_params=pltpu.CompilerParams(vmem_limit_bytes=FULL_VMEM),
        cost_estimate=pl.CostEstimate(flops=2_400_000_000, bytes_accessed=24 << 20, transcendentals=200_000),
        name="attend",
    )(
        hbm(hidden.reshape(ROWS, width)), hbm(query_weight), hbm(output_weight), hbm(kv_pool),
        hbm(new_kv.reshape(2 * ROWS, HD)), hbm(lengths), hbm(table), hbm(lengths.reshape(1, REQS)), hbm(freq),
    )

    def shift(k):
        return [(s, (s // RING) * RING + (s + k) % RING) for s in range(2 * RING)]

    def small(kernel, out, name, **specs):
        return pl.pallas_call(
            kernel,
            out_shape=out,
            **specs,
            compiler_params=pltpu.CompilerParams(vmem_limit_bytes=SMALL_VMEM),
            cost_estimate=pl.CostEstimate(flops=0, bytes_accessed=2 << 20, transcendentals=0),
            name=name,
        )

    far1 = lax.ppermute(far1, "tp", shift(1))
    far0 = lax.ppermute(far0, "tp", shift(-1))
    up0 = lax.ppermute(up0, "tp", shift(1))
    down1 = lax.ppermute(down1, "tp", shift(-1))
    next_up, next_down = small(relay_kernel, (piece,) * 2, "relay")(up1, down0, far1, far0)
    up1 = lax.ppermute(next_up, "tp", shift(1))
    down0 = lax.ppermute(next_down, "tp", shift(-1))
    half_piece = jax.ShapeDtypeStruct((ROWS // 2, share), BF16)
    keep, pass_on, near0, near1, far0, far1 = small(
        close_kernel, (piece,) * 2 + (half_piece,) * 4, "close"
    )(own, up0, up1, down0, down1, pick)
    flip_y = [(s, (s + RING) % (2 * RING)) for s in range(2 * RING)]
    flip_far = [(s, s ^ 8) for s in range(INST)]
    both = [
        (i * 2 * RING + s, (i ^ 8) * 2 * RING + (s + RING) % (2 * RING))
        for i in range(INST) for s in range(2 * RING)
    ]
    far0 = lax.ppermute(far0, "inst", flip_far)
    near1 = lax.ppermute(near1, "tp", flip_y)
    far1 = lax.ppermute(far1, ("inst", "tp"), both)
    same, cross = small(join_kernel, (half_piece,) * 2, "join")(near0, near1, far0, far1)
    other = lax.ppermute(pass_on, "tp", flip_y)
    crossed = lax.ppermute(cross, "inst", [(s, s ^ 1) for s in range(INST)])
    ahead = small(
        split_kernel, (jax.ShapeDtypeStruct((ROWS // RING, share), BF16),) * RING, "split"
    )(same, crossed)

    def along(k):
        return [(s, (s & 9) + (((s >> 1) + k) & (RING - 1)) * 2) for s in range(INST)]

    ahead = [ahead[0]] + [lax.ppermute(ahead[k], "inst", along(k)) for k in range(1, RING)]
    home = small(home_kernel, piece, "home")(keep, other, pick)
    arrival_cache = small(
        keep_kernel, pltpu.HBM(arrival_cache.shape, BF16), "keep_pages",
        in_specs=[ANY] * 2, out_specs=ANY, scratch_shapes=[pltpu.SemaphoreType.DMA((LANES,))],
    )(arrival_cache, hbm(home))
    arrival = small(arrive_kernel, piece, "arrive", in_specs=[VMEM] * RING + [ANY])(*ahead, hbm(arrival_cache))
    return (
        home.reshape(STEPS, REQS, share),
        arrival.reshape(STEPS, INST * CAP, share),
        arrival_cache,
    )


def solution(mesh):
    in_specs = (
        P(None, "inst", None),
        P(None, "tp"),
        P("tp", None),
        P("inst", None, None, "tp"),
        P(None, "inst", None, "tp"),
        P("inst"),
        P("inst", None),
        P("inst"),
        P("inst", None),
        P("inst"),
    )
    out_specs = (P(None, "inst", "tp"), P(None, "inst", "tp"), P("inst", None, None, None, "tp"))
    return jax.shard_map(local, mesh=mesh, in_specs=in_specs, out_specs=out_specs, check_vma=False)
```

```python
import functools

import jax
import jax.numpy as jnp
import numpy as np
from jax import lax
from jax.experimental import pallas as pl
from jax.experimental.pallas import tpu as pltpu
from jax.sharding import PartitionSpec as P

HD = 128
GROUP = 4
CAP = 2
STEPS = 4
REQS = 32
MIG = 16
INST = 16
PAGE = 64
MAXP = 3
RING = 4
SPAN = MAXP * PAGE
ROWS = STEPS * REQS
WIDE = 256
LANES = 8
ROPE_BASE = 500000.0
FULL_VMEM = 48 << 20
SMALL_VMEM = 6 << 20
F32 = jnp.float32
BF16 = jnp.bfloat16
SMEM = pl.BlockSpec(memory_space=pltpu.SMEM)
VMEM = pl.BlockSpec(memory_space=pltpu.VMEM)
ANY = pl.BlockSpec(memory_space=pl.ANY)


def pack_kernel(
    page_list, req_list, dest_list, resume_list, pool, send, pick,
    table, mreq, mdest, resume, slot_of, filled, count, kv, zeros, wide, kv_sem, sem, small_sem,
):
    size = pool.shape[0] // LANES
    load = [
        pltpu.make_async_copy(pool.at[pl.ds(i * size, size)], kv.at[pl.ds(i * size, size)], kv_sem.at[i])
        for i in range(LANES)
    ]
    small = [
        pltpu.make_async_copy(source, target, small_sem.at[i])
        for i, (source, target) in enumerate((
            (req_list, mreq), (dest_list, mdest), (resume_list, resume), (page_list, table),
        ))
    ]
    for copy in small:
        copy.start()
    for copy in load:
        copy.start()
    zeros[...] = jnp.zeros_like(zeros)
    for s in range(INST * CAP):
        filled[s] = 0
    for d in range(INST):
        count[d] = 0
    for copy in small:
        copy.wait()
    for k in range(MIG):
        d = mdest[k]
        c = count[d]
        count[d] = c + 1
        slot_of[k] = d * CAP + c
        filled[d * CAP + c] = 1

    def clear(s, carry):
        @pl.when(filled[s] == 0)
        def _():
            pltpu.make_async_copy(zeros, send.at[s], sem).start()

        return carry

    lax.fori_loop(0, INST * CAP, clear, 0)
    for copy in load:
        copy.wait()
    for k in range(MIG):
        for p in range(MAXP):
            pltpu.make_async_copy(kv.at[table[p, mreq[k]]], send.at[slot_of[k], p], sem).start()

    here_at = lax.axis_index("inst")
    rows = lax.broadcasted_iota(jnp.int32, (2 * ROWS, ROWS), 0)
    cols = lax.broadcasted_iota(jnp.int32, (2 * ROWS, ROWS), 1)
    wide[...] = jnp.where(rows == cols, 1.0, 0.0).astype(F32)
    lane = lax.broadcasted_iota(jnp.int32, (1, ROWS), 1)
    for k in range(MIG):
        slot = slot_of[k]
        d, c = slot >> 1, slot & 1
        req = mreq[k]
        first = resume[k]
        far = (d >> 3) ^ (here_at >> 3)
        cross = (d ^ here_at) & 1
        ahead = ((d >> 1) - (here_at >> 1)) & (RING - 1)
        block = ROWS + far * (ROWS // 2) + cross * (ROWS // 4) + ahead * (STEPS * CAP)
        for t in range(STEPS):
            at = t * REQS + req
            wide[pl.ds(at, 1), :] = jnp.where((lane == at) & (t < first), 1.0, 0.0).astype(F32)
            wide[pl.ds(block + t * CAP + c, 1), :] = jnp.where((lane == at) & (t >= first), 1.0, 0.0).astype(F32)
    pick[...] = wide[...].astype(BF16)
    pltpu.make_async_copy(send, send, sem).wait()


def attend_kernel(
    hidden, wq, wo, pool, new_kv, len_list, page_list, len_line, freq_line,
    far1, far0, up0, down1, up1, down0, own,
    x, q_w, o_w, kv, fresh, turned, scores, probs, mixed, acc,
    recent, lengths, table, len_row, freq,
    x_sem, q_sem, o_sem, kv_sem, small_sem,
):
    chunks = x_sem.shape[0]
    depth = x.shape[1] // chunks
    share = own.shape[-1]
    tp = lax.axis_index("tp")
    y, z = tp // RING, tp % RING

    def load(k):
        cut = pl.ds(k * depth, depth)
        return (
            pltpu.make_async_copy(hidden.at[:, cut], x.at[:, cut], x_sem.at[k]),
            pltpu.make_async_copy(wq.at[cut], q_w.at[cut], q_sem.at[k]),
        )

    small = [
        pltpu.make_async_copy(source, target, small_sem.at[i])
        for i, (source, target) in enumerate((
            (new_kv, recent), (len_line, len_row), (freq_line, freq), (len_list, lengths), (page_list, table),
        ))
    ]
    for k in range(chunks):
        for copy in load(k):
            copy.start()
        if k == 0:
            for copy in small:
                copy.start()
    kv_copy = pltpu.make_async_copy(pool, kv, kv_sem)
    order = [(2, 1), (2, 0), (1, 0), (3, 1), (1, 1), (3, 0), (0, 1), (0, 0)]
    into = (far1, far0, up0, down1, up1, down0, own.at[1], own.at[0])

    def weight(i):
        k, j = order[i]
        n = lax.rem(y + j, 2) * RING + lax.rem(z + k, RING)
        cut = pl.ds(pl.multiple_of(n * share, share), share)
        return pltpu.make_async_copy(wo.at[:, cut], o_w.at[i], o_sem.at[i])

    for copy in small:
        copy.wait()

    row = lax.broadcasted_iota(jnp.int32, (REQS * 16, ROWS * 2), 0)
    col = lax.broadcasted_iota(jnp.int32, (REQS * 16, ROWS * 2), 1)
    home = (row & 15) * (2 * REQS) + (row >> 4) * 2
    source = recent[...]
    for j in range(2):
        choice = jnp.where((col == home + j) & ((row & 15) < STEPS), 1.0, 0.0).astype(BF16)
        fresh[j] = jnp.dot(choice, source, preferred_element_type=F32).astype(BF16)

    at = lax.broadcasted_iota(jnp.int32, (ROWS, REQS), 0)
    req = lax.broadcasted_iota(jnp.int32, (ROWS, REQS), 1)
    base = jnp.sum(
        jnp.where((at & (REQS - 1)) == req, len_row[...].astype(F32), 0.0), axis=1, keepdims=True
    )
    step = (lax.broadcasted_iota(jnp.int32, (ROWS, 1), 0) >> 5).astype(F32)
    angles = (base + step) * freq[...]
    cos = jnp.cos(angles)
    sin = jnp.sin(angles)
    lane = lax.broadcasted_iota(jnp.int32, (ROWS, HD), 1)
    sin = jnp.where(lane < HD // 2, -sin, sin)

    for k in range(chunks):
        for copy in load(k):
            copy.wait()
        if k == 2:
            kv_copy.start()
        if k >= 4:
            for i in (2 * k - 8, 2 * k - 7):
                weight(i).start()
        cut = pl.ds(k * depth, depth)
        part = jnp.dot(x[:, cut], q_w[cut], preferred_element_type=F32)
        if k == 0:
            acc[...] = part
        else:
            acc[...] += part

    for g in range(GROUP):
        head = acc[:, g * HD:(g + 1) * HD]
        turned[g * ROWS:(g + 1) * ROWS] = head * cos + pltpu.roll(head, HD // 2, 1) * sin

    kv_copy.wait()
    scale = HD ** -0.5
    spot = lax.broadcasted_iota(jnp.int32, (16, WIDE), 1)
    when = lax.broadcasted_iota(jnp.int32, (16, WIDE), 0) & (STEPS - 1)
    causal = (spot >= SPAN) & (spot - SPAN <= when)
    rest = jnp.zeros((WIDE - SPAN - 16, HD), BF16)

    def pages(r, j):
        cached = [kv[table[p, r], j] for p in range(MAXP)]
        return jnp.concatenate(cached + [fresh[j, r * 16:(r + 1) * 16], rest], axis=0)

    for r in range(REQS):
        query = turned[pl.ds(r, 16, stride=REQS), :].astype(BF16)
        found = lax.dot_general(
            query, pages(r, 0), (((1,), (1,)), ((), ())), preferred_element_type=F32
        ) * scale
        live = (spot < lengths[r]) | causal
        scores[r * 16:(r + 1) * 16] = jnp.where(live, found, -1e30)

    held = scores[...]
    top = jnp.max(held, axis=1, keepdims=True)
    raised = jnp.exp(held - top)
    total = jnp.sum(raised, axis=1, keepdims=True)
    probs[...] = (raised * (1.0 / total)).astype(BF16)

    for r in range(REQS):
        mixed[pl.ds(r, 16, stride=REQS), :] = jnp.dot(
            probs[r * 16:(r + 1) * 16], pages(r, 1), preferred_element_type=F32
        )

    rows = jnp.concatenate(
        [mixed[g * ROWS:(g + 1) * ROWS].astype(BF16) for g in range(GROUP)], axis=1
    )
    for i in range(len(order)):
        weight(i).wait()
        into[i][...] = jnp.dot(rows, o_w[i], preferred_element_type=F32).astype(BF16)


def relay_kernel(up1, down0, far1, far0, next_up, next_down):
    next_up[...] = (up1[...].astype(F32) + far1[...].astype(F32)).astype(BF16)
    next_down[...] = (down0[...].astype(F32) + far0[...].astype(F32)).astype(BF16)


def close_kernel(
    own, up0, up1, down0, down1, pick, keep, pass_on, near0, near1, far0, far1
):
    choice = pick[ROWS:]
    mine = (own[0].astype(F32) + up0[...].astype(F32) + down0[...].astype(F32)).astype(BF16)
    other = (own[1].astype(F32) + up1[...].astype(F32) + down1[...].astype(F32)).astype(BF16)
    keep[...] = mine
    pass_on[...] = other
    for part, near, far in ((mine, near0, far0), (other, near1, far1)):
        taken = jnp.dot(choice, part, preferred_element_type=F32).astype(BF16)
        near[...] = taken[:ROWS // 2]
        far[...] = taken[ROWS // 2:]


def home_kernel(keep, other, pick, home):
    total = (keep[...].astype(F32) + other[...].astype(F32)).astype(BF16)
    home[...] = jnp.dot(pick[:ROWS], total, preferred_element_type=F32).astype(BF16)


def join_kernel(near0, near1, far0, far1, same, cross):
    near = (near0[...].astype(F32) + near1[...].astype(F32)).astype(BF16)
    far = (far0[...].astype(F32) + far1[...].astype(F32)).astype(BF16)
    to = lax.broadcasted_iota(jnp.int32, (ROWS, ROWS), 0)
    come = lax.broadcasted_iota(jnp.int32, (ROWS, ROWS), 1)
    source = ((to >> 3) & 1) * (ROWS // 2) + (to >> 4) * (STEPS * CAP) + (to & 7)
    turn = jnp.where(come == source, 1.0, 0.0).astype(BF16)
    rows = jnp.dot(turn, jnp.concatenate([near, far], axis=0), preferred_element_type=F32).astype(BF16)
    same[...] = rows[:ROWS // 2]
    cross[...] = rows[ROWS // 2:]


def split_kernel(same, crossed, *ahead):
    for k in range(RING):
        ahead[k][:16] = same[k * 16:(k + 1) * 16]
        ahead[k][16:] = crossed[k * 16:(k + 1) * 16]


def arrive_kernel(k0, k1, k3, k2, kept, out):
    here_at = lax.axis_index("inst")
    rows = jnp.concatenate([k0[...], k1[...], k2[...], k3[...]], axis=0)
    to = lax.broadcasted_iota(jnp.int32, (ROWS, ROWS), 0)
    come = lax.broadcasted_iota(jnp.int32, (ROWS, ROWS), 1)
    t, s, c = to >> 5, (to >> 1) & (INST - 1), to & (CAP - 1)
    behind = ((here_at >> 1) - (s >> 1)) & (RING - 1)
    cross = (s ^ here_at) & 1
    far = ((s ^ here_at) >> 3) & 1
    source = behind * 32 + cross * 16 + far * 8 + t * CAP + c
    turn = jnp.where(come == source, 1.0, 0.0).astype(BF16)
    out[...] = jnp.dot(turn, rows, preferred_element_type=F32).astype(BF16)


def keep_kernel(got, after, out, sem):
    size = got.shape[0] // LANES
    copies = [
        pltpu.make_async_copy(got.at[pl.ds(i * size, size)], out.at[pl.ds(i * size, size)], sem.at[i])
        for i in range(LANES)
    ]
    for copy in copies:
        copy.start()
    for copy in copies:
        copy.wait()


def local(
    hidden, query_weight, output_weight, kv_pool, new_kv,
    lengths, page_table, mig_req, mig_dest, resume,
):
    width = hidden.shape[-1]
    share = width // lax.axis_size("tp")
    table = page_table.T
    hbm = functools.partial(pltpu.with_memory_space_constraint, memory_space=pltpu.HBM)
    send, pick = pl.pallas_call(
        pack_kernel,
        out_shape=(
            pltpu.HBM((INST * CAP, MAXP) + kv_pool.shape[1:], BF16),
            jax.ShapeDtypeStruct((2 * ROWS, ROWS), BF16),
        ),
        in_specs=[ANY] * 5,
        out_specs=(ANY, VMEM),
        scratch_shapes=[
            pltpu.SMEM((MAXP, REQS), jnp.int32),
            pltpu.SMEM((MIG,), jnp.int32),
            pltpu.SMEM((MIG,), jnp.int32),
            pltpu.SMEM((MIG,), jnp.int32),
            pltpu.SMEM((MIG,), jnp.int32),
            pltpu.SMEM((INST * CAP,), jnp.int32),
            pltpu.SMEM((INST,), jnp.int32),
            pltpu.VMEM(kv_pool.shape, BF16),
            pltpu.VMEM((MAXP,) + kv_pool.shape[1:], BF16),
            pltpu.VMEM((2 * ROWS, ROWS), F32),
            pltpu.SemaphoreType.DMA((LANES,)),
            pltpu.SemaphoreType.DMA,
            pltpu.SemaphoreType.DMA((4,)),
        ],
        compiler_params=pltpu.CompilerParams(vmem_limit_bytes=FULL_VMEM),
        cost_estimate=pl.CostEstimate(flops=0, bytes_accessed=6 << 20, transcendentals=0),
        name="pack_pages",
    )(hbm(table), hbm(mig_req), hbm(mig_dest.reshape(-1)), hbm(resume), hbm(kv_pool))
    arrival_cache = lax.all_to_all(send, "inst", split_axis=0, concat_axis=0, tiled=True)

    half = HD // 2
    inverse = np.float32(ROPE_BASE) ** (-np.arange(half, dtype=np.float32) * np.float32(2.0) / np.float32(HD))
    freq = jnp.asarray(np.concatenate([inverse, inverse])[None, :].astype(np.float32))
    chunks = 8
    piece = jax.ShapeDtypeStruct((ROWS, share), BF16)
    far1, far0, up0, down1, up1, down0, own = pl.pallas_call(
        attend_kernel,
        out_shape=(pltpu.VMEM((ROWS, share), BF16),) * 6 + (pltpu.VMEM((2, ROWS, share), BF16),),
        in_specs=[ANY] * 9,
        out_specs=(VMEM,) * 7,
        scratch_shapes=[
            pltpu.VMEM((ROWS, width), BF16),
            pltpu.VMEM(query_weight.shape, BF16),
            pltpu.VMEM((2 * RING, GROUP * HD, share), BF16),
            pltpu.VMEM(kv_pool.shape, BF16),
            pltpu.VMEM((2, REQS * 16, HD), BF16),
            pltpu.VMEM((GROUP * ROWS, HD), F32),
            pltpu.VMEM((REQS * 16, WIDE), F32),
            pltpu.VMEM((REQS * 16, WIDE), BF16),
            pltpu.VMEM((GROUP * ROWS, HD), F32),
            pltpu.VMEM((ROWS, GROUP * HD), F32),
            pltpu.VMEM((2 * ROWS, HD), BF16),
            pltpu.SMEM((REQS,), jnp.int32),
            pltpu.SMEM((MAXP, REQS), jnp.int32),
            pltpu.VMEM((1, REQS), jnp.int32),
            pltpu.VMEM((1, HD), F32),
            pltpu.SemaphoreType.DMA((chunks,)),
            pltpu.SemaphoreType.DMA((chunks,)),
            pltpu.SemaphoreType.DMA((2 * RING,)),
            pltpu.SemaphoreType.DMA,
            pltpu.SemaphoreType.DMA((5,)),
        ],
        compiler_params=pltpu.CompilerParams(vmem_limit_bytes=FULL_VMEM),
        cost_estimate=pl.CostEstimate(flops=2_400_000_000, bytes_accessed=24 << 20, transcendentals=200_000),
        name="attend",
    )(
        hbm(hidden.reshape(ROWS, width)), hbm(query_weight), hbm(output_weight), hbm(kv_pool),
        hbm(new_kv.reshape(2 * ROWS, HD)), hbm(lengths), hbm(table), hbm(lengths.reshape(1, REQS)), hbm(freq),
    )

    def shift(k):
        return [(s, (s // RING) * RING + (s + k) % RING) for s in range(2 * RING)]

    def small(kernel, out, name, **specs):
        return pl.pallas_call(
            kernel,
            out_shape=out,
            **specs,
            compiler_params=pltpu.CompilerParams(vmem_limit_bytes=SMALL_VMEM),
            cost_estimate=pl.CostEstimate(flops=0, bytes_accessed=2 << 20, transcendentals=0),
            name=name,
        )

    far1 = lax.ppermute(far1, "tp", shift(1))
    far0 = lax.ppermute(far0, "tp", shift(-1))
    up0 = lax.ppermute(up0, "tp", shift(1))
    down1 = lax.ppermute(down1, "tp", shift(-1))
    next_up, next_down = small(relay_kernel, (piece,) * 2, "relay")(up1, down0, far1, far0)
    up1 = lax.ppermute(next_up, "tp", shift(1))
    down0 = lax.ppermute(next_down, "tp", shift(-1))
    half_piece = jax.ShapeDtypeStruct((ROWS // 2, share), BF16)
    keep, pass_on, near0, near1, far0, far1 = small(
        close_kernel, (piece,) * 2 + (half_piece,) * 4, "close"
    )(own, up0, up1, down0, down1, pick)
    flip_y = [(s, (s + RING) % (2 * RING)) for s in range(2 * RING)]
    flip_far = [(s, s ^ 8) for s in range(INST)]
    both = [
        (i * 2 * RING + s, (i ^ 8) * 2 * RING + (s + RING) % (2 * RING))
        for i in range(INST) for s in range(2 * RING)
    ]
    far0 = lax.ppermute(far0, "inst", flip_far)
    near1 = lax.ppermute(near1, "tp", flip_y)
    far1 = lax.ppermute(far1, ("inst", "tp"), both)
    same, cross = small(join_kernel, (half_piece,) * 2, "join")(near0, near1, far0, far1)
    other = lax.ppermute(pass_on, "tp", flip_y)
    crossed = lax.ppermute(cross, "inst", [(s, s ^ 1) for s in range(INST)])
    ahead = small(
        split_kernel, (jax.ShapeDtypeStruct((ROWS // RING, share), BF16),) * RING, "split"
    )(same, crossed)

    def along(k):
        return [(s, (s & 9) + (((s >> 1) + k) & (RING - 1)) * 2) for s in range(INST)]

    ahead = [ahead[0]] + [lax.ppermute(ahead[k], "inst", along(k)) for k in (1, 3, 2)]
    home = small(home_kernel, piece, "home")(keep, other, pick)
    arrival_cache = small(
        keep_kernel, pltpu.HBM(arrival_cache.shape, BF16), "keep_pages",
        in_specs=[ANY] * 2, out_specs=ANY, scratch_shapes=[pltpu.SemaphoreType.DMA((LANES,))],
    )(arrival_cache, hbm(home))
    arrival = small(arrive_kernel, piece, "arrive", in_specs=[VMEM] * RING + [ANY])(*ahead, hbm(arrival_cache))
    return (
        home.reshape(STEPS, REQS, share),
        arrival.reshape(STEPS, INST * CAP, share),
        arrival_cache,
    )


def solution(mesh):
    in_specs = (
        P(None, "inst", None),
        P(None, "tp"),
        P("tp", None),
        P("inst", None, None, "tp"),
        P(None, "inst", None, "tp"),
        P("inst"),
        P("inst", None),
        P("inst"),
        P("inst", None),
        P("inst"),
    )
    out_specs = (P(None, "inst", "tp"), P(None, "inst", "tp"), P("inst", None, None, None, "tp"))
    return jax.shard_map(local, mesh=mesh, in_specs=in_specs, out_specs=out_specs, check_vma=False)
```

```python
import functools

import jax
import jax.numpy as jnp
import numpy as np
from jax import lax
from jax.experimental import pallas as pl
from jax.experimental.pallas import tpu as pltpu
from jax.sharding import PartitionSpec as P

HD = 128
GROUP = 4
CAP = 2
STEPS = 4
REQS = 32
MIG = 16
INST = 16
PAGE = 64
MAXP = 3
RING = 4
SPAN = MAXP * PAGE
ROWS = STEPS * REQS
WIDE = 256
LANES = 8
ROPE_BASE = 500000.0
FULL_VMEM = 48 << 20
SMALL_VMEM = 6 << 20
F32 = jnp.float32
BF16 = jnp.bfloat16
SMEM = pl.BlockSpec(memory_space=pltpu.SMEM)
VMEM = pl.BlockSpec(memory_space=pltpu.VMEM)
ANY = pl.BlockSpec(memory_space=pl.ANY)


def pack_kernel(
    page_list, req_list, dest_list, pool, send,
    table, mreq, mdest, slot_of, filled, count, kv, zeros, kv_sem, sem, small_sem,
):
    size = pool.shape[0] // LANES
    load = [
        pltpu.make_async_copy(pool.at[pl.ds(i * size, size)], kv.at[pl.ds(i * size, size)], kv_sem.at[i])
        for i in range(LANES)
    ]
    small = [
        pltpu.make_async_copy(source, target, small_sem.at[i])
        for i, (source, target) in enumerate((
            (req_list, mreq), (dest_list, mdest), (page_list, table),
        ))
    ]
    for copy in small:
        copy.start()
    for copy in load:
        copy.start()
    zeros[...] = jnp.zeros_like(zeros)
    for s in range(INST * CAP):
        filled[s] = 0
    for d in range(INST):
        count[d] = 0
    for copy in small:
        copy.wait()
    for k in range(MIG):
        d = mdest[k]
        c = count[d]
        count[d] = c + 1
        slot_of[k] = d * CAP + c
        filled[d * CAP + c] = 1

    def clear(s, carry):
        @pl.when(filled[s] == 0)
        def _():
            pltpu.make_async_copy(zeros, send.at[s], sem).start()

        return carry

    lax.fori_loop(0, INST * CAP, clear, 0)
    for copy in load:
        copy.wait()
    for k in range(MIG):
        for p in range(MAXP):
            pltpu.make_async_copy(kv.at[table[p, mreq[k]]], send.at[slot_of[k], p], sem).start()

    pltpu.make_async_copy(send, send, sem).wait()


def choose_kernel(mreq, mdest, resume, pick, count, wide):
    for d in range(INST):
        count[d] = 0
    here_at = lax.axis_index("inst")
    rows = lax.broadcasted_iota(jnp.int32, (2 * ROWS, ROWS), 0)
    cols = lax.broadcasted_iota(jnp.int32, (2 * ROWS, ROWS), 1)
    wide[...] = jnp.where(rows == cols, 1.0, 0.0).astype(F32)
    lane = lax.broadcasted_iota(jnp.int32, (1, ROWS), 1)
    for k in range(MIG):
        d = mdest[k]
        c = count[d]
        count[d] = c + 1
        req = mreq[k]
        first = resume[k]
        far = (d >> 3) ^ (here_at >> 3)
        cross = (d ^ here_at) & 1
        ahead = ((d >> 1) - (here_at >> 1)) & (RING - 1)
        block = ROWS + far * (ROWS // 2) + cross * (ROWS // 4) + ahead * (STEPS * CAP)
        for t in range(STEPS):
            at = t * REQS + req
            wide[pl.ds(at, 1), :] = jnp.where((lane == at) & (t < first), 1.0, 0.0).astype(F32)
            wide[pl.ds(block + t * CAP + c, 1), :] = jnp.where((lane == at) & (t >= first), 1.0, 0.0).astype(F32)
    pick[...] = wide[...].astype(BF16)


def attend_kernel(
    hidden, wq, wo, pool, new_kv, len_list, page_list, len_line, freq_line,
    far1, far0, up0, down1, up1, down0, own,
    x, q_w, o_w, kv, fresh, turned, scores, probs, mixed, acc,
    recent, lengths, table, len_row, freq,
    x_sem, q_sem, o_sem, kv_sem, small_sem,
):
    chunks = x_sem.shape[0]
    depth = x.shape[1] // chunks
    share = own.shape[-1]
    tp = lax.axis_index("tp")
    y, z = tp // RING, tp % RING

    def load(k):
        cut = pl.ds(k * depth, depth)
        return (
            pltpu.make_async_copy(hidden.at[:, cut], x.at[:, cut], x_sem.at[k]),
            pltpu.make_async_copy(wq.at[cut], q_w.at[cut], q_sem.at[k]),
        )

    small = [
        pltpu.make_async_copy(source, target, small_sem.at[i])
        for i, (source, target) in enumerate((
            (new_kv, recent), (len_line, len_row), (freq_line, freq), (len_list, lengths), (page_list, table),
        ))
    ]
    for k in range(chunks):
        for copy in load(k):
            copy.start()
        if k == 0:
            for copy in small:
                copy.start()
    kv_copy = pltpu.make_async_copy(pool, kv, kv_sem)
    order = [(2, 1), (2, 0), (1, 0), (3, 1), (1, 1), (3, 0), (0, 1), (0, 0)]
    into = (far1, far0, up0, down1, up1, down0, own.at[1], own.at[0])

    def weight(i):
        k, j = order[i]
        n = lax.rem(y + j, 2) * RING + lax.rem(z + k, RING)
        cut = pl.ds(pl.multiple_of(n * share, share), share)
        return pltpu.make_async_copy(wo.at[:, cut], o_w.at[i], o_sem.at[i])

    for copy in small:
        copy.wait()

    row = lax.broadcasted_iota(jnp.int32, (REQS * 16, ROWS * 2), 0)
    col = lax.broadcasted_iota(jnp.int32, (REQS * 16, ROWS * 2), 1)
    home = (row & 15) * (2 * REQS) + (row >> 4) * 2
    source = recent[...]
    for j in range(2):
        choice = jnp.where((col == home + j) & ((row & 15) < STEPS), 1.0, 0.0).astype(BF16)
        fresh[j] = jnp.dot(choice, source, preferred_element_type=F32).astype(BF16)

    at = lax.broadcasted_iota(jnp.int32, (ROWS, REQS), 0)
    req = lax.broadcasted_iota(jnp.int32, (ROWS, REQS), 1)
    base = jnp.sum(
        jnp.where((at & (REQS - 1)) == req, len_row[...].astype(F32), 0.0), axis=1, keepdims=True
    )
    step = (lax.broadcasted_iota(jnp.int32, (ROWS, 1), 0) >> 5).astype(F32)
    angles = (base + step) * freq[...]
    cos = jnp.cos(angles)
    sin = jnp.sin(angles)
    lane = lax.broadcasted_iota(jnp.int32, (ROWS, HD), 1)
    sin = jnp.where(lane < HD // 2, -sin, sin)

    for k in range(chunks):
        for copy in load(k):
            copy.wait()
        if k == 2:
            kv_copy.start()
        if k >= 4:
            for i in (2 * k - 8, 2 * k - 7):
                weight(i).start()
        cut = pl.ds(k * depth, depth)
        part = jnp.dot(x[:, cut], q_w[cut], preferred_element_type=F32)
        if k == 0:
            acc[...] = part
        else:
            acc[...] += part

    for g in range(GROUP):
        head = acc[:, g * HD:(g + 1) * HD]
        turned[g * ROWS:(g + 1) * ROWS] = head * cos + pltpu.roll(head, HD // 2, 1) * sin

    kv_copy.wait()
    scale = HD ** -0.5
    spot = lax.broadcasted_iota(jnp.int32, (16, WIDE), 1)
    when = lax.broadcasted_iota(jnp.int32, (16, WIDE), 0) & (STEPS - 1)
    causal = (spot >= SPAN) & (spot - SPAN <= when)
    rest = jnp.zeros((WIDE - SPAN - 16, HD), BF16)

    def pages(r, j):
        cached = [kv[table[p, r], j] for p in range(MAXP)]
        return jnp.concatenate(cached + [fresh[j, r * 16:(r + 1) * 16], rest], axis=0)

    for r in range(REQS):
        query = turned[pl.ds(r, 16, stride=REQS), :].astype(BF16)
        found = lax.dot_general(
            query, pages(r, 0), (((1,), (1,)), ((), ())), preferred_element_type=F32
        ) * scale
        live = (spot < lengths[r]) | causal
        scores[r * 16:(r + 1) * 16] = jnp.where(live, found, -1e30)

    held = scores[...]
    top = jnp.max(held, axis=1, keepdims=True)
    raised = jnp.exp(held - top)
    total = jnp.sum(raised, axis=1, keepdims=True)
    probs[...] = (raised * (1.0 / total)).astype(BF16)

    for r in range(REQS):
        mixed[pl.ds(r, 16, stride=REQS), :] = jnp.dot(
            probs[r * 16:(r + 1) * 16], pages(r, 1), preferred_element_type=F32
        )

    rows = jnp.concatenate(
        [mixed[g * ROWS:(g + 1) * ROWS].astype(BF16) for g in range(GROUP)], axis=1
    )
    for i in range(len(order)):
        weight(i).wait()
        into[i][...] = jnp.dot(rows, o_w[i], preferred_element_type=F32).astype(BF16)


def relay_kernel(up1, down0, far1, far0, next_up, next_down):
    next_up[...] = (up1[...].astype(F32) + far1[...].astype(F32)).astype(BF16)
    next_down[...] = (down0[...].astype(F32) + far0[...].astype(F32)).astype(BF16)


def close_kernel(
    own, up0, up1, down0, down1, pick, keep, pass_on, near0, near1, far0, far1
):
    choice = pick[ROWS:]
    mine = (own[0].astype(F32) + up0[...].astype(F32) + down0[...].astype(F32)).astype(BF16)
    other = (own[1].astype(F32) + up1[...].astype(F32) + down1[...].astype(F32)).astype(BF16)
    keep[...] = mine
    pass_on[...] = other
    for part, near, far in ((mine, near0, far0), (other, near1, far1)):
        taken = jnp.dot(choice, part, preferred_element_type=F32).astype(BF16)
        near[...] = taken[:ROWS // 2]
        far[...] = taken[ROWS // 2:]


def home_kernel(keep, other, pick, home):
    total = (keep[...].astype(F32) + other[...].astype(F32)).astype(BF16)
    home[...] = jnp.dot(pick[:ROWS], total, preferred_element_type=F32).astype(BF16)


def join_kernel(near0, near1, far0, far1, same, cross):
    near = (near0[...].astype(F32) + near1[...].astype(F32)).astype(BF16)
    far = (far0[...].astype(F32) + far1[...].astype(F32)).astype(BF16)
    to = lax.broadcasted_iota(jnp.int32, (ROWS, ROWS), 0)
    come = lax.broadcasted_iota(jnp.int32, (ROWS, ROWS), 1)
    source = ((to >> 3) & 1) * (ROWS // 2) + (to >> 4) * (STEPS * CAP) + (to & 7)
    turn = jnp.where(come == source, 1.0, 0.0).astype(BF16)
    rows = jnp.dot(turn, jnp.concatenate([near, far], axis=0), preferred_element_type=F32).astype(BF16)
    same[...] = rows[:ROWS // 2]
    cross[...] = rows[ROWS // 2:]


def split_kernel(same, crossed, *ahead):
    for k in range(RING):
        ahead[k][:16] = same[k * 16:(k + 1) * 16]
        ahead[k][16:] = crossed[k * 16:(k + 1) * 16]


def arrive_kernel(k0, k1, k3, k2, kept, out):
    here_at = lax.axis_index("inst")
    rows = jnp.concatenate([k0[...], k1[...], k2[...], k3[...]], axis=0)
    to = lax.broadcasted_iota(jnp.int32, (ROWS, ROWS), 0)
    come = lax.broadcasted_iota(jnp.int32, (ROWS, ROWS), 1)
    t, s, c = to >> 5, (to >> 1) & (INST - 1), to & (CAP - 1)
    behind = ((here_at >> 1) - (s >> 1)) & (RING - 1)
    cross = (s ^ here_at) & 1
    far = ((s ^ here_at) >> 3) & 1
    source = behind * 32 + cross * 16 + far * 8 + t * CAP + c
    turn = jnp.where(come == source, 1.0, 0.0).astype(BF16)
    out[...] = jnp.dot(turn, rows, preferred_element_type=F32).astype(BF16)


def keep_kernel(got, after, out, sem):
    size = got.shape[0] // LANES
    copies = [
        pltpu.make_async_copy(got.at[pl.ds(i * size, size)], out.at[pl.ds(i * size, size)], sem.at[i])
        for i in range(LANES)
    ]
    for copy in copies:
        copy.start()
    for copy in copies:
        copy.wait()


def local(
    hidden, query_weight, output_weight, kv_pool, new_kv,
    lengths, page_table, mig_req, mig_dest, resume,
):
    width = hidden.shape[-1]
    share = width // lax.axis_size("tp")
    table = page_table.T
    hbm = functools.partial(pltpu.with_memory_space_constraint, memory_space=pltpu.HBM)
    send = pl.pallas_call(
        pack_kernel,
        out_shape=pltpu.HBM((INST * CAP, MAXP) + kv_pool.shape[1:], BF16),
        in_specs=[ANY] * 4,
        out_specs=ANY,
        scratch_shapes=[
            pltpu.SMEM((MAXP, REQS), jnp.int32),
            pltpu.SMEM((MIG,), jnp.int32),
            pltpu.SMEM((MIG,), jnp.int32),
            pltpu.SMEM((MIG,), jnp.int32),
            pltpu.SMEM((INST * CAP,), jnp.int32),
            pltpu.SMEM((INST,), jnp.int32),
            pltpu.VMEM(kv_pool.shape, BF16),
            pltpu.VMEM((MAXP,) + kv_pool.shape[1:], BF16),
            pltpu.SemaphoreType.DMA((LANES,)),
            pltpu.SemaphoreType.DMA,
            pltpu.SemaphoreType.DMA((3,)),
        ],
        compiler_params=pltpu.CompilerParams(vmem_limit_bytes=FULL_VMEM),
        cost_estimate=pl.CostEstimate(flops=0, bytes_accessed=6 << 20, transcendentals=0),
        name="pack_pages",
    )(hbm(table), hbm(mig_req), hbm(mig_dest.reshape(-1)), hbm(kv_pool))
    arrival_cache = lax.all_to_all(send, "inst", split_axis=0, concat_axis=0, tiled=True)

    half = HD // 2
    inverse = np.float32(ROPE_BASE) ** (-np.arange(half, dtype=np.float32) * np.float32(2.0) / np.float32(HD))
    freq = jnp.asarray(np.concatenate([inverse, inverse])[None, :].astype(np.float32))
    chunks = 8
    piece = jax.ShapeDtypeStruct((ROWS, share), BF16)
    far1, far0, up0, down1, up1, down0, own = pl.pallas_call(
        attend_kernel,
        out_shape=(pltpu.VMEM((ROWS, share), BF16),) * 6 + (pltpu.VMEM((2, ROWS, share), BF16),),
        in_specs=[ANY] * 9,
        out_specs=(VMEM,) * 7,
        scratch_shapes=[
            pltpu.VMEM((ROWS, width), BF16),
            pltpu.VMEM(query_weight.shape, BF16),
            pltpu.VMEM((2 * RING, GROUP * HD, share), BF16),
            pltpu.VMEM(kv_pool.shape, BF16),
            pltpu.VMEM((2, REQS * 16, HD), BF16),
            pltpu.VMEM((GROUP * ROWS, HD), F32),
            pltpu.VMEM((REQS * 16, WIDE), F32),
            pltpu.VMEM((REQS * 16, WIDE), BF16),
            pltpu.VMEM((GROUP * ROWS, HD), F32),
            pltpu.VMEM((ROWS, GROUP * HD), F32),
            pltpu.VMEM((2 * ROWS, HD), BF16),
            pltpu.SMEM((REQS,), jnp.int32),
            pltpu.SMEM((MAXP, REQS), jnp.int32),
            pltpu.VMEM((1, REQS), jnp.int32),
            pltpu.VMEM((1, HD), F32),
            pltpu.SemaphoreType.DMA((chunks,)),
            pltpu.SemaphoreType.DMA((chunks,)),
            pltpu.SemaphoreType.DMA((2 * RING,)),
            pltpu.SemaphoreType.DMA,
            pltpu.SemaphoreType.DMA((5,)),
        ],
        compiler_params=pltpu.CompilerParams(vmem_limit_bytes=FULL_VMEM),
        cost_estimate=pl.CostEstimate(flops=2_400_000_000, bytes_accessed=24 << 20, transcendentals=200_000),
        name="attend",
    )(
        hbm(hidden.reshape(ROWS, width)), hbm(query_weight), hbm(output_weight), hbm(kv_pool),
        hbm(new_kv.reshape(2 * ROWS, HD)), hbm(lengths), hbm(table), hbm(lengths.reshape(1, REQS)), hbm(freq),
    )

    def shift(k):
        return [(s, (s // RING) * RING + (s + k) % RING) for s in range(2 * RING)]

    def small(kernel, out, name, **specs):
        return pl.pallas_call(
            kernel,
            out_shape=out,
            **specs,
            compiler_params=pltpu.CompilerParams(vmem_limit_bytes=SMALL_VMEM),
            cost_estimate=pl.CostEstimate(flops=0, bytes_accessed=2 << 20, transcendentals=0),
            name=name,
        )

    far1 = lax.ppermute(far1, "tp", shift(1))
    far0 = lax.ppermute(far0, "tp", shift(-1))
    up0 = lax.ppermute(up0, "tp", shift(1))
    down1 = lax.ppermute(down1, "tp", shift(-1))
    next_up, next_down = small(relay_kernel, (piece,) * 2, "relay")(up1, down0, far1, far0)
    up1 = lax.ppermute(next_up, "tp", shift(1))
    down0 = lax.ppermute(next_down, "tp", shift(-1))
    pick = small(
        choose_kernel, jax.ShapeDtypeStruct((2 * ROWS, ROWS), BF16), "choose", in_specs=[SMEM] * 3,
        scratch_shapes=[pltpu.SMEM((INST,), jnp.int32), pltpu.VMEM((2 * ROWS, ROWS), F32)],
    )(mig_req, mig_dest.reshape(-1), resume)
    half_piece = jax.ShapeDtypeStruct((ROWS // 2, share), BF16)
    keep, pass_on, near0, near1, far0, far1 = small(
        close_kernel, (piece,) * 2 + (half_piece,) * 4, "close"
    )(own, up0, up1, down0, down1, pick)
    flip_y = [(s, (s + RING) % (2 * RING)) for s in range(2 * RING)]
    flip_far = [(s, s ^ 8) for s in range(INST)]
    both = [
        (i * 2 * RING + s, (i ^ 8) * 2 * RING + (s + RING) % (2 * RING))
        for i in range(INST) for s in range(2 * RING)
    ]
    far0 = lax.ppermute(far0, "inst", flip_far)
    near1 = lax.ppermute(near1, "tp", flip_y)
    far1 = lax.ppermute(far1, ("inst", "tp"), both)
    same, cross = small(join_kernel, (half_piece,) * 2, "join")(near0, near1, far0, far1)
    other = lax.ppermute(pass_on, "tp", flip_y)
    crossed = lax.ppermute(cross, "inst", [(s, s ^ 1) for s in range(INST)])
    ahead = small(
        split_kernel, (jax.ShapeDtypeStruct((ROWS // RING, share), BF16),) * RING, "split"
    )(same, crossed)

    def along(k):
        return [(s, (s & 9) + (((s >> 1) + k) & (RING - 1)) * 2) for s in range(INST)]

    ahead = [ahead[0]] + [lax.ppermute(ahead[k], "inst", along(k)) for k in (1, 3, 2)]
    home = small(home_kernel, piece, "home")(keep, other, pick)
    arrival_cache = small(
        keep_kernel, pltpu.HBM(arrival_cache.shape, BF16), "keep_pages",
        in_specs=[ANY] * 2, out_specs=ANY, scratch_shapes=[pltpu.SemaphoreType.DMA((LANES,))],
    )(arrival_cache, hbm(home))
    arrival = small(arrive_kernel, piece, "arrive", in_specs=[VMEM] * RING + [ANY])(*ahead, hbm(arrival_cache))
    return (
        home.reshape(STEPS, REQS, share),
        arrival.reshape(STEPS, INST * CAP, share),
        arrival_cache,
    )


def solution(mesh):
    in_specs = (
        P(None, "inst", None),
        P(None, "tp"),
        P("tp", None),
        P("inst", None, None, "tp"),
        P(None, "inst", None, "tp"),
        P("inst"),
        P("inst", None),
        P("inst"),
        P("inst", None),
        P("inst"),
    )
    out_specs = (P(None, "inst", "tp"), P(None, "inst", "tp"), P("inst", None, None, None, "tp"))
    return jax.shard_map(local, mesh=mesh, in_specs=in_specs, out_specs=out_specs, check_vma=False)
```
